128 devices in a mesh: dp: 8 (over y, z_hi), ctx: 16 (over x, z_lo, core).
Axes of the slice: x: 4, y: 4, z: 4 (z_hi: 2, z_lo: 2; z = z_hi * 2 + z_lo), core: 2. Of those that a mesh axis runs over, the one named last changes fastest.
Arguments:
- query_rows: bfloat16 [65536, 2048], P(('dp', 'ctx')), may hold values from -6 to 6
- key_rows: bfloat16 [65536, 2048], P(('dp', 'ctx')), may hold values from -6 to 6
- value_rows: bfloat16 [65536, 2048], P(('dp', 'ctx')), may hold values from -6 to 6
- pyramid_start: int32 [65536], P(('dp', 'ctx')), may hold values from 0 to 8191, as said below
- scale_end: int32 [65536], P(('dp', 'ctx')), may hold values from 1 to 8192, as said below
- out_weight: bfloat16 [2048, 2048], P('dp'), may hold values from -0.125 to 0.125
- cotangent: bfloat16 [65536, 2048], P(('dp', 'ctx')), may hold values from -6 to 6
Outputs:
- layer_out: bfloat16 [65536, 2048], P(('dp', 'ctx'))
- query_grad: bfloat16 [65536, 2048], P(('dp', 'ctx'))
- key_grad: bfloat16 [65536, 2048], P(('dp', 'ctx'))
- value_grad: bfloat16 [65536, 2048], P(('dp', 'ctx'))
- weight_grad: float32 [2048, 2048], P('dp')
The draws below stay inside these ranges and needn't reach their ends.
Inputs may be any that keep to these rules, and one draw needn't show every extreme that they name: `pyramid_start`: each group's packed sequence of 8192 tokens is cut into pyramids laid end to end; a pyramid is the first 4 to 9 scales of lengths 1, 1, 4, 9, 16, 25, 36, 64, 100 (at most 256 tokens), a pyramid may be cut off at the group's end, the first pyramid of every group has 4 scales and the next 2 pyramids have all 9, and the group's last token always starts a pyramid of its own. Each token holds its pyramid's first position counted within its group. `scale_end`: each token holds one past the last position of its scale within its group, cut at 8191 for every token but the group's last; it is above the token's own position and at most 256 above its pyramid_start.
All inputs are finite; a program needn't handle non-finite values.
Results may differ from the reference program's by a relative error of at most 0.0072.
Values may be sent and summed in bfloat16 or wider, within the bound.
No kernel may reach another device: no remote copies, remote signals or barrier semaphores. Data moves between devices by JAX's collectives and lax.ppermute only.
A program may use at most 192 MiB of HBM per device.

```python
import jax
import jax.numpy as jnp
from jax import lax

HEADS = 16
HEAD_DIM = 128
DW = 2048
PYR = 256
TOK_DEV = 512
GROUP_LEN = 8192
GROUPS = 8
TOKENS = 65536
N_CTX = 16


def pyramid_bounds(key):
    level_ends = jnp.array([1, 2, 6, 15, 31, 56, 92, 156, 256], jnp.int32)
    pyramid_count = GROUP_LEN // 15 + 2
    full_count = TOK_DEV // PYR
    levels = jax.random.randint(key, (GROUPS, pyramid_count), 4, 10)
    levels = levels.at[:, 0].set(4)
    levels = levels.at[:, 1:1 + full_count].set(9)
    lengths = level_ends[levels - 1]
    finishes = jnp.cumsum(lengths, axis=1)
    starts = finishes - lengths
    position = jnp.arange(GROUP_LEN, dtype=jnp.int32)
    which = jax.vmap(lambda row: jnp.searchsorted(row, position, side='right') - 1)(starts)
    begin = jnp.take_along_axis(starts, which, axis=1)
    offset = position[None, :] - begin
    level_index = jnp.searchsorted(level_ends, offset, side='right')
    finish = jnp.minimum(begin + level_ends[level_index], GROUP_LEN - 1)
    begin = begin.at[:, GROUP_LEN - 1].set(GROUP_LEN - 1)
    finish = finish.at[:, GROUP_LEN - 1].set(GROUP_LEN)
    return (begin.reshape(-1).astype(jnp.int32), finish.reshape(-1).astype(jnp.int32))


def draw_pyramid_start(key, part):
    begin, finish = pyramid_bounds(key)
    return begin


def draw_scale_end(key, part):
    begin, finish = pyramid_bounds(key)
    return finish


def draw_query_rows(key, part):
    width = HEADS * HEAD_DIM
    key = jax.random.fold_in(key, 21)
    rows = jnp.clip(jax.random.normal(key, (TOKENS, width), jnp.float32), -6.0, 6.0)
    return rows.astype(jnp.bfloat16)


def draw_key_rows(key, part):
    width = HEADS * HEAD_DIM
    key = jax.random.fold_in(key, 22)
    rows = jnp.clip(jax.random.normal(key, (TOKENS, width), jnp.float32), -6.0, 6.0)
    return rows.astype(jnp.bfloat16)


def level_of(stream_key, shape, split, smallest, high):
    gain, own = 1.0, jax.random.fold_in(stream_key, 6)
    for dim, parts in split:
        draws = jnp.exp(jax.random.uniform(jax.random.fold_in(own, dim), (parts,), jnp.float32, smallest / len(split), high / len(split)))
        gain = gain * jnp.repeat(draws, shape[dim] // parts).reshape([-1 if axis == dim else 1 for axis in range(len(shape))])
    return gain


def gaussian(rng, shape, scale, limit, pieces=(), kind=jnp.bfloat16):
    level = level_of(rng, shape, pieces, -0.22, 0.18) if pieces else 1.0
    result = jax.random.normal(rng, shape, jnp.float32) * scale * level
    return jnp.minimum(jnp.maximum(result, -limit), limit).astype(kind)


def setup_inputs(seed: int = 0) -> dict:
    keys = jax.random.split(jax.random.key(seed), 8)
    return {
        "query_rows": draw_query_rows(jax.random.fold_in(keys[7], 71), 0),
        "key_rows": draw_key_rows(jax.random.fold_in(keys[7], 71), 0),
        "value_rows": gaussian(keys[2], (TOKENS, HEADS * HEAD_DIM), 1.0, 6.0, ((0, 128),)),
        "pyramid_start": draw_pyramid_start(jax.random.fold_in(keys[7], 71), 0),
        "scale_end": draw_scale_end(jax.random.fold_in(keys[7], 71), 0),
        "out_weight": gaussian(keys[5], (HEADS * HEAD_DIM, DW), (HEADS * HEAD_DIM) ** -0.5, 0.125, ((0, 8),)),
        "cotangent": gaussian(keys[6], (TOKENS, DW), 1.0, 6.0, ((0, 128),)),
    }


def low_copy(values):
    return lax.optimization_barrier(values.astype(jnp.bfloat16)).astype(jnp.float32)


def reference(query_rows, key_rows, value_rows, pyramid_start, scale_end, out_weight, cotangent):
    width = HEADS * HEAD_DIM
    factor = HEAD_DIM ** -0.5
    span = TOK_DEV + 2 * PYR
    grad_attn = jnp.dot(cotangent, out_weight.T, preferred_element_type=jnp.float32).astype(jnp.bfloat16)

    def pad_rows(array):
        grouped = array.reshape(GROUPS, GROUP_LEN, width)
        return jnp.pad(grouped, ((0, 0), (PYR, PYR), (0, 0)))

    key_pad = pad_rows(key_rows)
    value_pad = pad_rows(value_rows)
    zero_index = jnp.zeros((), jnp.int32)

    def step(carry, block):
        key_accum, value_accum = carry
        group = (block // N_CTX).astype(jnp.int32)
        first = ((block % N_CTX) * TOK_DEV).astype(jnp.int32)
        begin = (block * TOK_DEV).astype(jnp.int32)
        query_block = lax.dynamic_slice_in_dim(query_rows, begin, TOK_DEV, 0)
        grad_block = lax.dynamic_slice_in_dim(grad_attn, begin, TOK_DEV, 0)
        start_block = lax.dynamic_slice_in_dim(pyramid_start, begin, TOK_DEV, 0)
        end_block = lax.dynamic_slice_in_dim(scale_end, begin, TOK_DEV, 0)
        key_block = lax.dynamic_slice(key_pad, (group, first, zero_index), (1, span, width))[0]
        value_block = lax.dynamic_slice(value_pad, (group, first, zero_index), (1, span, width))[0]
        key_pos = first - PYR + jnp.arange(span, dtype=jnp.int32)
        allowed = (key_pos[None, :] >= start_block[:, None]) & (key_pos[None, :] < end_block[:, None])
        query_four = query_block.astype(jnp.float32).reshape(TOK_DEV, HEADS, HEAD_DIM)
        key_four = key_block.astype(jnp.float32).reshape(span, HEADS, HEAD_DIM)
        value_four = value_block.astype(jnp.float32).reshape(span, HEADS, HEAD_DIM)
        grad_four = grad_block.astype(jnp.float32).reshape(TOK_DEV, HEADS, HEAD_DIM)
        scores = jnp.einsum("qhd,khd->hqk", query_four, key_four) * factor
        scores = jnp.where(allowed[None], scores, -jnp.inf)
        top = jnp.max(scores, axis=2, keepdims=True)
        weights = jnp.exp(scores - top)
        probs = weights / jnp.sum(weights, axis=2, keepdims=True)
        probs_low = low_copy(probs)
        mixed = jnp.einsum("hqk,khd->qhd", probs_low, value_four).astype(jnp.bfloat16).reshape(TOK_DEV, width)
        grad_values = jnp.einsum("hqk,qhd->khd", probs_low, grad_four).reshape(span, width)
        grad_probs = jnp.einsum("qhd,khd->hqk", grad_four, value_four)
        inner = jnp.sum(probs * grad_probs, axis=2, keepdims=True)
        grad_scores = low_copy(probs * (grad_probs - inner))
        grad_query = (jnp.einsum("hqk,khd->qhd", grad_scores, key_four) * factor).astype(jnp.bfloat16).reshape(TOK_DEV, width)
        grad_keys = (jnp.einsum("hqk,qhd->khd", grad_scores, query_four) * factor).reshape(span, width)
        old_keys = lax.dynamic_slice(key_accum, (group, first, zero_index), (1, span, width))
        old_values = lax.dynamic_slice(value_accum, (group, first, zero_index), (1, span, width))
        key_accum = lax.dynamic_update_slice(key_accum, old_keys + grad_keys[None], (group, first, zero_index))
        value_accum = lax.dynamic_update_slice(value_accum, old_values + grad_values[None], (group, first, zero_index))
        return (key_accum, value_accum), (mixed, grad_query)

    empty = jnp.zeros((GROUPS, GROUP_LEN + 2 * PYR, width), jnp.float32)
    blocks = jnp.arange(TOKENS // TOK_DEV, dtype=jnp.int32)
    (key_accum, value_accum), (mixed, grad_query) = lax.scan(step, (empty, empty), blocks)
    attn = mixed.reshape(TOKENS, width)
    query_grad = grad_query.reshape(TOKENS, width)
    key_grad = key_accum[:, PYR:PYR + GROUP_LEN].reshape(TOKENS, width).astype(jnp.bfloat16)
    value_grad = value_accum[:, PYR:PYR + GROUP_LEN].reshape(TOKENS, width).astype(jnp.bfloat16)
    layer_out = jnp.dot(attn, out_weight, preferred_element_type=jnp.float32).astype(jnp.bfloat16)
    weight_grad = lax.dot_general(attn, cotangent, (((0,), (0,)), ((), ())), preferred_element_type=jnp.float32) * (TOKENS ** -0.5)
    return layer_out, query_grad, key_grad, value_grad, weight_grad
```

```python
import functools

import jax
import jax.numpy as jnp
from jax import lax
from jax.experimental import pallas as pl
from jax.experimental.pallas import tpu as pltpu
from jax.sharding import Mesh, PartitionSpec as P

HEADS = 16
HEAD_DIM = 128
WIDTH = HEADS * HEAD_DIM
TOK = 512
BLOCK = 256
BEFORE = 256
AFTER = 128
SPAN = BEFORE + BLOCK + AFTER
FACTOR = HEAD_DIM ** -0.5
TOKENS = 65536

AXES = ("y", "zh", "x", "zl", "core")
SIZES = (4, 2, 4, 2, 2)
GROUP_AXES = ("x", "zl", "core")
CHIPS = ("y", "zh", "x", "zl")
SHARDS = 8
MB = 1024 * 1024
PER_STEP = 4
STEPS = HEADS // PER_STEP
COLS = PER_STEP * HEAD_DIM


def dot_nt(left, right):
    return lax.dot_general(left, right, (((1,), (1,)), ((), ())), preferred_element_type=jnp.float32)


def dot_nn(left, right):
    return lax.dot_general(left, right, (((1,), (0,)), ((), ())), preferred_element_type=jnp.float32)


def dot_tn(left, right):
    return lax.dot_general(left, right, (((0,), (0,)), ((), ())), preferred_element_type=jnp.float32)


def fixed(shape):
    return pl.BlockSpec(shape, lambda i, *_: (0,) * len(shape))


def columns(rows, shift=0, row_block=0):
    return pl.BlockSpec((rows, COLS), lambda i, *_: (row_block, i + shift))


def cost(flops, micros=0.0):
    return pl.CostEstimate(flops=int(flops), bytes_accessed=int(micros * 3.0e6), transcendentals=0)


def params(mib):
    return pltpu.CompilerParams(vmem_limit_bytes=mib * MB)


def fill_bias(late, start_ref, end_ref, bias_ref):
    first = 0 if late else -BEFORE
    pos = lax.broadcasted_iota(jnp.int32, (SPAN, BLOCK), 0) + first
    ok = (pos >= start_ref[...]) & (pos < end_ref[...])
    bias_ref[...] = jnp.where(ok, 0.0, -jnp.inf).astype(jnp.float32)


def gather_keys(late, own, halo):
    if late:
        return jnp.concatenate([own, halo], axis=0)
    return jnp.concatenate([halo, own[: SPAN - BEFORE]], axis=0)


def forward_kernel(core_ref, start_ref, end_ref, q_ref, ko_ref, kh_ref, vo_ref, vh_ref,
                   out_ref, theirs_ref, lse_ref, bias_ref, *, late):
    @pl.when(pl.program_id(0) == 0)
    def _():
        fill_bias(late, start_ref, end_ref, bias_ref)

    even = core_ref[0] == 0
    for pair in range(PER_STEP // 2):
        outs = []
        for h in (2 * pair, 2 * pair + 1):
            cols = slice(h * HEAD_DIM, (h + 1) * HEAD_DIM)
            k = gather_keys(late, ko_ref[:, cols], kh_ref[:, cols])
            v = gather_keys(late, vo_ref[:, cols], vh_ref[:, cols])
            s = dot_nt(k, q_ref[:, cols]) + bias_ref[...]
            top = jnp.max(s, axis=0, keepdims=True)
            e = jnp.exp((s - top) * FACTOR)
            total = jnp.sum(e, axis=0, keepdims=True)
            o_t = dot_nn(v.T, e.astype(jnp.bfloat16)) * (1.0 / total)
            out = o_t.T.astype(jnp.bfloat16)
            out_ref[:, cols] = out
            outs.append(out)
            lse_ref[h] = top * FACTOR + jnp.log(total)
        theirs_ref[:, pair * HEAD_DIM:(pair + 1) * HEAD_DIM] = jnp.where(even, outs[1], outs[0])


def forward(late, core, start, end, q, k, v, halo):
    row_block = 1 if late else 0
    halo_rows = AFTER if late else BEFORE
    bounds = pl.BlockSpec((1, BLOCK), lambda i, *_: (0, row_block))
    return pl.pallas_call(
        functools.partial(forward_kernel, late=late),
        grid_spec=pltpu.PrefetchScalarGridSpec(
            num_scalar_prefetch=1,
            grid=(STEPS,),
            in_specs=[bounds, bounds, columns(BLOCK, row_block=row_block),
                      columns(TOK), columns(halo_rows), columns(TOK), columns(halo_rows, STEPS)],
            out_specs=[columns(BLOCK),
                       pl.BlockSpec((BLOCK, COLS // 2), lambda i, *_: (0, i)),
                       pl.BlockSpec((PER_STEP, 1, BLOCK), lambda i, *_: (i, 0, 0))],
            scratch_shapes=[pltpu.VMEM((SPAN, BLOCK), jnp.float32)],
        ),
        out_shape=[jax.ShapeDtypeStruct((BLOCK, WIDTH), jnp.bfloat16),
                   jax.ShapeDtypeStruct((BLOCK, WIDTH // 2), jnp.bfloat16),
                   jax.ShapeDtypeStruct((HEADS, 1, BLOCK), jnp.float32)],
        compiler_params=params(32),
        cost_estimate=cost(10e9),
        name="attend_late" if late else "attend_early",
    )(core, start, end, q, k, halo, v, halo)


def backward_kernel(start_ref, end_ref, lse_ref, q_ref, g_ref, ko_ref, kh_ref, vo_ref, vh_ref, *refs, late):
    if late:
        dki_ref, dvi_ref, dq_ref, dk_ref, dv_ref, halo_k_ref, halo_v_ref, bias_ref = refs
    else:
        dq_ref, dk_ref, dv_ref, halo_k_ref, halo_v_ref, bias_ref = refs

    @pl.when(pl.program_id(0) == 0)
    def _():
        fill_bias(late, start_ref, end_ref, bias_ref)

    for h in range(PER_STEP):
        cols = slice(h * HEAD_DIM, (h + 1) * HEAD_DIM)
        k = gather_keys(late, ko_ref[:, cols], kh_ref[:, cols])
        v = gather_keys(late, vo_ref[:, cols], vh_ref[:, cols])
        q = q_ref[:, cols]
        g = g_ref[:, cols]
        s = dot_nt(k, q) + bias_ref[...]
        p = jnp.exp(s * FACTOR - lse_ref[h])
        dp = dot_nt(v, g)
        inner = jnp.sum(p * dp, axis=0, keepdims=True)
        ds = (p * (dp - inner)).astype(jnp.bfloat16)
        dv = dot_nn(p.astype(jnp.bfloat16), g)
        dk = dot_nn(ds, q) * FACTOR
        dq_ref[:, cols] = (dot_nn(k.T, ds) * FACTOR).T.astype(jnp.bfloat16)
        if late:
            keep = SPAN - BEFORE
            dk_ref[:keep, cols] = (dk[:keep] + dki_ref[:, cols].astype(jnp.float32)).astype(jnp.bfloat16)
            dv_ref[:keep, cols] = (dv[:keep] + dvi_ref[:, cols].astype(jnp.float32)).astype(jnp.bfloat16)
            dk_ref[keep:, cols] = dk[keep:TOK].astype(jnp.bfloat16)
            dv_ref[keep:, cols] = dv[keep:TOK].astype(jnp.bfloat16)
            halo_k_ref[:, cols] = dk[TOK:].astype(jnp.bfloat16)
            halo_v_ref[:, cols] = dv[TOK:].astype(jnp.bfloat16)
        else:
            dk_ref[:, cols] = dk[BEFORE:].astype(dk_ref.dtype)
            dv_ref[:, cols] = dv[BEFORE:].astype(dv_ref.dtype)
            halo_k_ref[:, cols] = dk[:BEFORE].astype(jnp.bfloat16)
            halo_v_ref[:, cols] = dv[:BEFORE].astype(jnp.bfloat16)


def backward(late, start, end, lse, q, g, k, v, halo, *earlier):
    row_block = 1 if late else 0
    halo_rows = AFTER if late else BEFORE
    own_rows = TOK if late else SPAN - BEFORE
    own_type = jnp.bfloat16 if late else jnp.float32
    bounds = pl.BlockSpec((1, BLOCK), lambda i, *_: (0, row_block))
    shape = jax.ShapeDtypeStruct
    return pl.pallas_call(
        functools.partial(backward_kernel, late=late),
        grid=(STEPS,),
        in_specs=[bounds, bounds, pl.BlockSpec((PER_STEP, 1, BLOCK), lambda i: (i, 0, 0)),
                  columns(BLOCK, row_block=row_block), columns(BLOCK, row_block=row_block),
                  columns(TOK), columns(halo_rows), columns(TOK), columns(halo_rows, STEPS)]
        + [columns(SPAN - BEFORE)] * len(earlier),
        out_specs=[columns(BLOCK), columns(own_rows), columns(own_rows), columns(halo_rows), columns(halo_rows)],
        out_shape=[shape((BLOCK, WIDTH), jnp.bfloat16),
                   shape((own_rows, WIDTH), own_type), shape((own_rows, WIDTH), own_type),
                   shape((halo_rows, WIDTH), jnp.bfloat16), shape((halo_rows, WIDTH), jnp.bfloat16)],
        scratch_shapes=[pltpu.VMEM((SPAN, BLOCK), jnp.float32)],
        compiler_params=params(40),
        cost_estimate=cost(13e9),
        name="grads_late" if late else "grads_early",
    )(start, end, lse, q, g, k, halo, v, halo, *earlier)


def finish_kernel(dq0_ref, dq1_ref, dk_ref, dv_ref, kn_ref, vn_ref, kp_ref, vp_ref, dq_ref, dko_ref, dvo_ref):
    dq_ref[:BLOCK] = dq0_ref[...]
    dq_ref[BLOCK:] = dq1_ref[...]
    for own_ref, next_ref, prev_ref, out_ref in ((dk_ref, kn_ref, kp_ref, dko_ref), (dv_ref, vn_ref, vp_ref, dvo_ref)):
        f32 = jnp.float32
        out_ref[:AFTER] = (own_ref[:AFTER].astype(f32) + prev_ref[...].astype(f32)).astype(jnp.bfloat16)
        out_ref[AFTER:TOK - BEFORE] = own_ref[AFTER:TOK - BEFORE]
        out_ref[TOK - BEFORE:] = (own_ref[TOK - BEFORE:].astype(f32) + next_ref[...].astype(f32)).astype(jnp.bfloat16)


def finish(dq0, dq1, dk, dv, k_next, v_next, k_prev, v_prev):
    return pl.pallas_call(
        finish_kernel,
        grid=(STEPS,),
        in_specs=[columns(BLOCK), columns(BLOCK), columns(TOK), columns(TOK),
                  columns(BEFORE), columns(BEFORE), columns(AFTER), columns(AFTER)],
        out_specs=[columns(TOK)] * 3,
        out_shape=[jax.ShapeDtypeStruct((TOK, WIDTH), jnp.bfloat16)] * 3,
        compiler_params=params(24),
        cost_estimate=cost(4e9),
        name="finish_grads",
    )(dq0, dq1, dk, dv, k_next, v_next, k_prev, v_prev)


def weight_sums_kernel(core_ref, early_ref, late_ref, peer_early_ref, peer_late_ref, cot_ref, cot_peer_ref, out_ref):
    own = jnp.concatenate([early_ref[...], late_ref[...]], axis=0)
    peer = jnp.concatenate([peer_early_ref[...], peer_late_ref[...]], axis=0)
    core = core_ref[0]
    parts = [jnp.where(core == 0, own[:, 2 * j * HEAD_DIM:(2 * j + 1) * HEAD_DIM],
                       own[:, (2 * j + 1) * HEAD_DIM:(2 * j + 2) * HEAD_DIM]) for j in range(2)]
    own = jnp.concatenate(parts, axis=1)
    both = dot_tn(own, cot_ref[...]) + dot_tn(peer, cot_peer_ref[...])
    out_ref[...] = both.astype(jnp.bfloat16)


def weight_sums(core, early, late, peer_early, peer_late, cot, cot_peer):
    own_spec = pl.BlockSpec((BLOCK, 4 * HEAD_DIM), lambda i, *_: (0, i))
    peer_spec = pl.BlockSpec((BLOCK, 2 * HEAD_DIM), lambda i, *_: (0, i))
    return pl.pallas_call(
        weight_sums_kernel,
        grid_spec=pltpu.PrefetchScalarGridSpec(
            num_scalar_prefetch=1,
            grid=(4,),
            in_specs=[own_spec, own_spec, peer_spec, peer_spec, fixed((TOK, WIDTH)), fixed((TOK, WIDTH))],
            out_specs=pl.BlockSpec((2 * HEAD_DIM, WIDTH), lambda i, *_: (i, 0)),
        ),
        out_shape=jax.ShapeDtypeStruct((WIDTH // 2, WIDTH), jnp.bfloat16),
        compiler_params=params(40),
        cost_estimate=cost(7e9),
        name="weight_sums",
    )(core, early, late, peer_early, peer_late, cot, cot_peer)


def grad_attn_kernel(core_ref, cot_ref, mine_ref, other_ref, out_ref, rows_ref):
    core = core_ref[0]
    rows_ref[core] = mine_ref[0]
    rows_ref[1 - core] = other_ref[0]
    out_ref[...] = dot_nt(cot_ref[...], rows_ref[...].reshape(2 * HEAD_DIM, WIDTH)).astype(jnp.bfloat16)


def grad_attention(core, cot, mine, other):
    piece = pl.BlockSpec((1, HEAD_DIM, WIDTH), lambda i, *_: (i, 0, 0))
    return pl.pallas_call(
        grad_attn_kernel,
        grid_spec=pltpu.PrefetchScalarGridSpec(
            num_scalar_prefetch=1,
            grid=(SHARDS,),
            in_specs=[fixed((TOK, WIDTH)), piece, piece],
            out_specs=pl.BlockSpec((TOK, 2 * HEAD_DIM), lambda i, *_: (0, i)),
            scratch_shapes=[pltpu.VMEM((2, HEAD_DIM, WIDTH), jnp.bfloat16)],
        ),
        out_shape=jax.ShapeDtypeStruct((TOK, WIDTH), jnp.bfloat16),
        compiler_params=params(32),
        cost_estimate=cost(7e9),
        name="grad_attention",
    )(core, cot, mine, other)


def project_kernel(core_ref, early_ref, late_ref, mine_ref, other_ref, out_ref, rows_ref):
    core = core_ref[0]
    tile = out_ref.shape[1]
    rows_ref[:, core] = mine_ref[...]
    rows_ref[:, 1 - core] = other_ref[...]
    weight = rows_ref[...].reshape(WIDTH, tile)
    out_ref[:BLOCK] = dot_nn(early_ref[...], weight).astype(jnp.bfloat16)
    out_ref[BLOCK:] = dot_nn(late_ref[...], weight).astype(jnp.bfloat16)


def project(core, early, late, mine, other):
    tile = 512
    piece = pl.BlockSpec((SHARDS, HEAD_DIM, tile), lambda i, *_: (0, 0, i))
    return pl.pallas_call(
        project_kernel,
        grid_spec=pltpu.PrefetchScalarGridSpec(
            num_scalar_prefetch=1,
            grid=(WIDTH // tile,),
            in_specs=[fixed((BLOCK, WIDTH)), fixed((BLOCK, WIDTH)), piece, piece],
            out_specs=pl.BlockSpec((TOK, tile), lambda i, *_: (0, i)),
            scratch_shapes=[pltpu.VMEM((SHARDS, 2, HEAD_DIM, tile), jnp.bfloat16)],
        ),
        out_shape=jax.ShapeDtypeStruct((TOK, WIDTH), jnp.bfloat16),
        compiler_params=params(32),
        cost_estimate=cost(7e9),
        name="project",
    )(core, early, late, mine, other)


def sum_pieces_kernel(pieces_ref, out_ref):
    total = pieces_ref[0].astype(jnp.float32)
    for i in range(1, pieces_ref.shape[0]):
        total += pieces_ref[i].astype(jnp.float32)
    for i in range(out_ref.shape[0]):
        out_ref[i] = total.astype(jnp.bfloat16)


def sum_pieces(pieces, copies):
    count, rows, width = pieces.shape
    tile = 512
    return pl.pallas_call(
        sum_pieces_kernel,
        grid=(width // tile,),
        in_specs=[pl.BlockSpec((count, rows, tile), lambda i: (0, 0, i))],
        out_specs=pl.BlockSpec((copies, rows, tile), lambda i: (0, 0, i)),
        out_shape=jax.ShapeDtypeStruct((copies, rows, width), jnp.bfloat16),
        compiler_params=params(24),
        cost_estimate=cost(2e9),
        name="sum_pieces",
    )(pieces)


def swapped(array):
    return lax.ppermute(array, "core", [(0, 1), (1, 0)])


def passed_along(array, by):
    devices = 16
    pairs = [(i, i + by) for i in range(devices) if 0 <= i + by < devices]
    return lax.ppermute(array, GROUP_AXES, pairs)


def on_device(query_rows, key_rows, value_rows, pyramid_start, scale_end, out_weight, cotangent):
    core = lax.axis_index("core").astype(jnp.int32)
    group_index = lax.axis_index(GROUP_AXES).astype(jnp.int32)
    core_arg = core.reshape(1)
    start = (pyramid_start - group_index * TOK).reshape(1, TOK)
    end = (scale_end - group_index * TOK).reshape(1, TOK)

    after = passed_along(jnp.concatenate([key_rows[:AFTER], value_rows[:AFTER]], axis=1), -1)
    before = passed_along(jnp.concatenate([key_rows[TOK - BEFORE:], value_rows[TOK - BEFORE:]], axis=1), 1)
    half = lax.dynamic_slice_in_dim(out_weight, core * HEAD_DIM, HEAD_DIM, 0)
    mine = lax.all_to_all(jnp.broadcast_to(half, (SHARDS, HEAD_DIM, WIDTH)), ("y", "zh"), 0, 0, tiled=True)
    other = swapped(mine)
    cot_peer = swapped(cotangent)

    late, late_theirs, late_lse = forward(True, core_arg, start, end, query_rows, key_rows, value_rows, after)
    peer_late = swapped(late_theirs)
    early, early_theirs, early_lse = forward(False, core_arg, start, end, query_rows, key_rows, value_rows, before)
    peer_early = swapped(early_theirs)

    sums = weight_sums(core_arg, early, late, peer_early, peer_late, cotangent, cot_peer)
    pieces = lax.all_to_all(sums.reshape(64, 16, WIDTH), CHIPS, 0, 0, tiled=True)

    grad_attn = grad_attention(core_arg, cotangent, mine, other)
    dq0, dk0, dv0, k_before, v_before = backward(
        False, start, end, early_lse, query_rows, grad_attn, key_rows, value_rows, before)
    k_next = passed_along(k_before, -1)
    v_next = passed_along(v_before, -1)
    dq1, dk1, dv1, k_after, v_after = backward(
        True, start, end, late_lse, query_rows, grad_attn, key_rows, value_rows, after, dk0, dv0)
    k_prev = passed_along(k_after, 1)
    v_prev = passed_along(v_after, 1)

    layer_out = project(core_arg, early, late, mine, other)

    summed = sum_pieces(pieces, 16)
    rows = lax.all_to_all(summed, ("core", "x", "zl"), 0, 0, tiled=True)
    weight_grad = rows.reshape(2 * HEAD_DIM, WIDTH).astype(jnp.float32) * (float(TOKENS) ** -0.5)

    query_grad, key_grad, value_grad = finish(dq0, dq1, dk1, dv1, k_next, v_next, k_prev, v_prev)
    return (layer_out, query_grad, key_grad, value_grad, weight_grad)


def solution(mesh):
    inner = Mesh(mesh.devices.reshape(SIZES), AXES)
    rows = P(AXES, None)
    shard = P(("y", "zh"), None)
    return jax.shard_map(
        on_device,
        mesh=inner,
        in_specs=(rows, rows, rows, P(AXES), P(AXES), shard, rows),
        out_specs=(rows, rows, rows, rows, shard),
        check_vma=False,
    )
```

```python
import functools

import jax
import jax.numpy as jnp
from jax import lax
from jax.experimental import pallas as pl
from jax.experimental.pallas import tpu as pltpu
from jax.sharding import Mesh, PartitionSpec as P

HEADS = 16
HEAD_DIM = 128
WIDTH = HEADS * HEAD_DIM
TOK = 512
BLOCK = 256
BEFORE = 256
AFTER = 128
SPAN = BEFORE + BLOCK + AFTER
FACTOR = HEAD_DIM ** -0.5
TOKENS = 65536

AXES = ("y", "zh", "x", "zl", "core")
SIZES = (4, 2, 4, 2, 2)
GROUP_AXES = ("x", "zl", "core")
MB = 1024 * 1024
PER_STEP = 4
STEPS = HEADS // PER_STEP
COLS = PER_STEP * HEAD_DIM


def dot_nt(left, right):
    return lax.dot_general(left, right, (((1,), (1,)), ((), ())), preferred_element_type=jnp.float32)


def dot_nn(left, right):
    return lax.dot_general(left, right, (((1,), (0,)), ((), ())), preferred_element_type=jnp.float32)


def dot_tn(left, right):
    return lax.dot_general(left, right, (((0,), (0,)), ((), ())), preferred_element_type=jnp.float32)


def fixed(shape):
    return pl.BlockSpec(shape, lambda i, *_: (0,) * len(shape))


def columns(rows, shift=0, row_block=0):
    return pl.BlockSpec((rows, COLS), lambda i, *_: (row_block, i + shift))


def halo_columns(rows):
    return pl.BlockSpec((2, rows, COLS), lambda i, *_: (0, 0, i))


def cost(flops):
    return pl.CostEstimate(flops=int(flops * 1e-3), bytes_accessed=0, transcendentals=0)


def params():
    return pltpu.CompilerParams(vmem_limit_bytes=56 * MB)


def fill_bias(late, start_ref, end_ref, bias_ref):
    first = 0 if late else -BEFORE
    pos = lax.broadcasted_iota(jnp.int32, (SPAN, BLOCK), 0) + first
    ok = (pos >= start_ref[...]) & (pos < end_ref[...])
    bias_ref[...] = jnp.where(ok, 0.0, -jnp.inf).astype(jnp.float32)


def gather_keys(late, own, halo):
    if late:
        return jnp.concatenate([own, halo], axis=0)
    return jnp.concatenate([halo, own[: SPAN - BEFORE]], axis=0)


HALVES = ((slice(0, 128), slice(0, 512)), (slice(128, 256), slice(128, 640)))


def assemble(first, second):
    none = jnp.zeros((SPAN - 512, 128), first.dtype)
    return jnp.concatenate([jnp.concatenate([first, none], axis=0), jnp.concatenate([none, second], axis=0)], axis=1)


def forward_kernel(core_ref, start_ref, end_ref, q_ref, ko_ref, kh_ref, vo_ref, vh_ref,
                   out_ref, theirs_ref, lse_ref, bias_ref, *, late):
    @pl.when(pl.program_id(0) == 0)
    def _():
        fill_bias(late, start_ref, end_ref, bias_ref)

    even = core_ref[0] == 0
    outs = []

    def head(h):
        return slice(h * HEAD_DIM, (h + 1) * HEAD_DIM)

    def scores(h):
        return dot_nt(gather_keys(late, ko_ref[:, head(h)], kh_ref[:, head(h)]), q_ref[:, head(h)])

    def weigh(s):
        parts = []
        for queries, keys in HALVES:
            part = s[keys, queries] + bias_ref[keys, queries]
            top = jnp.max(part, axis=0, keepdims=True)
            e = jnp.exp((part - top) * FACTOR)
            total = jnp.sum(e, axis=0, keepdims=True)
            parts.append((e.astype(jnp.bfloat16), top, total))
        first, second = parts
        return (assemble(first[0], second[0]), jnp.concatenate([first[1], second[1]], axis=1),
                jnp.concatenate([first[2], second[2]], axis=1))

    def mix(h, e, top, total):
        v = gather_keys(late, vo_ref[:, head(h)], vh_ref[:, head(h)])
        out = (dot_nn(v.T, e) * (1.0 / total)).T.astype(jnp.bfloat16)
        out_ref[:, head(h)] = out
        lse_ref[h] = top * FACTOR + jnp.log(total)
        outs.append(out)
        if h % 2:
            theirs_ref[:, head(h // 2)] = jnp.where(even, outs[h], outs[h - 1])

    ahead = scores(0)
    behind = None
    for h in range(PER_STEP):
        now, ahead = ahead, scores(h + 1) if h + 1 < PER_STEP else None
        weighed = weigh(now)
        if behind is not None:
            mix(h - 1, *behind)
        behind = weighed
    mix(PER_STEP - 1, *behind)


def forward(late, core, start, end, q, k, v, halo):
    row_block = 1 if late else 0
    halo_rows = AFTER if late else BEFORE
    bounds = pl.BlockSpec((1, BLOCK), lambda i, *_: (0, row_block))
    return pl.pallas_call(
        functools.partial(forward_kernel, late=late),
        grid_spec=pltpu.PrefetchScalarGridSpec(
            num_scalar_prefetch=1,
            grid=(STEPS,),
            in_specs=[bounds, bounds, columns(BLOCK, row_block=row_block),
                      columns(TOK), columns(halo_rows), columns(TOK), columns(halo_rows, STEPS)],
            out_specs=[columns(BLOCK),
                       pl.BlockSpec((BLOCK, COLS // 2), lambda i, *_: (0, i)),
                       pl.BlockSpec((PER_STEP, 1, BLOCK), lambda i, *_: (i, 0, 0))],
            scratch_shapes=[pltpu.VMEM((SPAN, BLOCK), jnp.float32)],
        ),
        out_shape=[jax.ShapeDtypeStruct((BLOCK, WIDTH), jnp.bfloat16),
                   jax.ShapeDtypeStruct((BLOCK, WIDTH // 2), jnp.bfloat16),
                   jax.ShapeDtypeStruct((HEADS, 1, BLOCK), jnp.float32)],
        compiler_params=params(),
        cost_estimate=cost(8e9),
        name="attend_late" if late else "attend_early",
    )(core, start, end, q, k, halo, v, halo)


def backward_kernel(place_ref, start_ref, end_ref, lse_ref, q_ref, near_ref, far_ref, ko_ref, kh_ref, vo_ref, vh_ref,
                    *refs, late):
    if late:
        dki_ref, dvi_ref, _, dq_ref, dk_ref, dv_ref, halo_ref, bias_ref, g_ref = refs
    else:
        dq_ref, dk_ref, dv_ref, halo_ref, bias_ref, g_ref = refs
    first = place_ref[1] == 0
    g_ref[:, :2 * HEAD_DIM] = jnp.where(first, near_ref[...], far_ref[...])
    g_ref[:, 2 * HEAD_DIM:] = jnp.where(first, far_ref[...], near_ref[...])

    @pl.when(pl.program_id(0) == 0)
    def _():
        fill_bias(late, start_ref, end_ref, bias_ref)

    def head(h):
        return slice(h * HEAD_DIM, (h + 1) * HEAD_DIM)

    def products(h):
        k = gather_keys(late, ko_ref[:, head(h)], kh_ref[:, head(h)])
        v = gather_keys(late, vo_ref[:, head(h)], vh_ref[:, head(h)])
        return k, [(dot_nt(k[keys], q_ref[queries, head(h)]), dot_nt(v[keys], g_ref[queries, head(h)]))
                   for queries, keys in HALVES]

    def differentiate(h, k, pairs):
        probs = []
        grads = []
        for (queries, keys), (s, dp) in zip(HALVES, pairs):
            p = jnp.exp((s + bias_ref[keys, queries]) * FACTOR - lse_ref[h, :, queries])
            inner = jnp.sum(p * dp, axis=0, keepdims=True)
            probs.append(p.astype(jnp.bfloat16))
            grads.append((p * (dp - inner)).astype(jnp.bfloat16))
        return k, assemble(*probs), assemble(*grads)

    def collect(h, k, p, ds):
        cols = head(h)
        dv = dot_nn(p, g_ref[:, cols])
        dk = dot_nn(ds, q_ref[:, cols]) * FACTOR
        dq_ref[:, cols] = (dot_nn(k.T, ds) * FACTOR).T.astype(jnp.bfloat16)
        if late:
            keep = SPAN - BEFORE
            dk_ref[:keep, cols] = (dk[:keep] + dki_ref[:, cols].astype(jnp.float32)).astype(jnp.bfloat16)
            dv_ref[:keep, cols] = (dv[:keep] + dvi_ref[:, cols].astype(jnp.float32)).astype(jnp.bfloat16)
            dk_ref[keep:, cols] = dk[keep:TOK].astype(jnp.bfloat16)
            dv_ref[keep:, cols] = dv[keep:TOK].astype(jnp.bfloat16)
            halo_ref[0, :, cols] = dk[TOK:].astype(jnp.bfloat16)
            halo_ref[1, :, cols] = dv[TOK:].astype(jnp.bfloat16)
        else:
            dk_ref[:, cols] = dk[BEFORE:].astype(dk_ref.dtype)
            dv_ref[:, cols] = dv[BEFORE:].astype(dv_ref.dtype)
            halo_ref[0, :, cols] = dk[:BEFORE].astype(jnp.bfloat16)
            halo_ref[1, :, cols] = dv[:BEFORE].astype(jnp.bfloat16)

    ahead = products(0)
    behind = None
    for h in range(PER_STEP):
        now, ahead = ahead, products(h + 1) if h + 1 < PER_STEP else None
        done = differentiate(h, *now)
        if behind is not None:
            collect(h - 1, *behind)
        behind = done
    collect(PER_STEP - 1, *behind)


def backward(late, place, start, end, lse, q, near, far, k, v, halo, *earlier):
    row_block = 1 if late else 0
    halo_rows = AFTER if late else BEFORE
    own_rows = TOK if late else SPAN - BEFORE
    own_type = jnp.bfloat16 if late else jnp.float32
    bounds = pl.BlockSpec((1, BLOCK), lambda i, *_: (0, row_block))
    half = pl.BlockSpec((BLOCK, COLS // 2), lambda i, *_: (row_block, i))
    shape = jax.ShapeDtypeStruct
    return pl.pallas_call(
        functools.partial(backward_kernel, late=late),
        grid_spec=pltpu.PrefetchScalarGridSpec(
            num_scalar_prefetch=1,
            grid=(STEPS,),
            in_specs=[bounds, bounds, pl.BlockSpec((PER_STEP, 1, BLOCK), lambda i, *_: (i, 0, 0)),
                      columns(BLOCK, row_block=row_block), half, half,
                      columns(TOK), columns(halo_rows), columns(TOK), columns(halo_rows, STEPS)]
            + ([columns(SPAN - BEFORE)] * 2 + [pl.BlockSpec(memory_space=pl.ANY)] if late else []),
            out_specs=[columns(BLOCK, row_block=row_block), columns(own_rows), columns(own_rows), halo_columns(halo_rows)],
            scratch_shapes=[pltpu.VMEM((SPAN, BLOCK), jnp.float32), pltpu.VMEM((BLOCK, COLS), jnp.bfloat16)],
        ),
        out_shape=[shape((TOK, WIDTH), jnp.bfloat16),
                   shape((own_rows, WIDTH), own_type), shape((own_rows, WIDTH), own_type),
                   shape((2, halo_rows, WIDTH), jnp.bfloat16)],
        input_output_aliases={13: 0} if late else {},
        compiler_params=params(),
        cost_estimate=cost(10e9),
        name="grads_late" if late else "grads_early",
    )(place, start, end, lse, q, near, far, k, halo, v, halo, *earlier)


def finish_kernel(dk_ref, dv_ref, next_ref, prev_ref, dko_ref, dvo_ref):
    f32 = jnp.float32
    for i, own_ref, out_ref in ((0, dk_ref, dko_ref), (1, dv_ref, dvo_ref)):
        out_ref[:AFTER] = (own_ref[:AFTER].astype(f32) + prev_ref[i].astype(f32)).astype(jnp.bfloat16)
        out_ref[AFTER:TOK - BEFORE] = own_ref[AFTER:TOK - BEFORE]
        out_ref[TOK - BEFORE:] = (own_ref[TOK - BEFORE:].astype(f32) + next_ref[i].astype(f32)).astype(jnp.bfloat16)


def finish(dk, dv, from_next, from_prev):
    return pl.pallas_call(
        finish_kernel,
        grid=(STEPS,),
        in_specs=[columns(TOK), columns(TOK), halo_columns(BEFORE), halo_columns(AFTER)],
        out_specs=[columns(TOK)] * 2,
        out_shape=[jax.ShapeDtypeStruct((TOK, WIDTH), jnp.bfloat16)] * 2,
        compiler_params=params(),
        cost_estimate=cost(4e9),
        name="finish_grads",
    )(dk, dv, from_next, from_prev)


def weight_sums_kernel(core_ref, early_ref, late_ref, peer_early_ref, peer_late_ref, cot_ref, cot_peer_ref, out_ref):
    own = jnp.concatenate([early_ref[...], late_ref[...]], axis=0)
    peer = jnp.concatenate([peer_early_ref[...], peer_late_ref[...]], axis=0)
    core = core_ref[0]
    parts = [jnp.where(core == 0, own[:, 2 * j * HEAD_DIM:(2 * j + 1) * HEAD_DIM],
                       own[:, (2 * j + 1) * HEAD_DIM:(2 * j + 2) * HEAD_DIM]) for j in range(2)]
    own = jnp.concatenate(parts, axis=1)
    out_ref[...] = (dot_tn(own, cot_ref[...]) + dot_tn(peer, cot_peer_ref[...])).astype(jnp.bfloat16)


def weight_sums(core, early, late, peer_early, peer_late, cot, cot_peer):
    own_spec = pl.BlockSpec((BLOCK, 4 * HEAD_DIM), lambda i, *_: (0, i))
    peer_spec = pl.BlockSpec((BLOCK, 2 * HEAD_DIM), lambda i, *_: (0, i))
    return pl.pallas_call(
        weight_sums_kernel,
        grid_spec=pltpu.PrefetchScalarGridSpec(
            num_scalar_prefetch=1,
            grid=(4,),
            in_specs=[own_spec, own_spec, peer_spec, peer_spec, fixed((TOK, WIDTH)), fixed((TOK, WIDTH))],
            out_specs=pl.BlockSpec((2 * HEAD_DIM, WIDTH), lambda i, *_: (i, 0)),
        ),
        out_shape=jax.ShapeDtypeStruct((WIDTH // 2, WIDTH), jnp.bfloat16),
        compiler_params=params(),
        cost_estimate=cost(7e9),
        name="weight_sums",
    )(core, early, late, peer_early, peer_late, cot, cot_peer)


def grad_attn_kernel(place_ref, cot_ref, mine_ref, other_ref, out_ref, rows_ref):
    core = place_ref[0]
    rows_ref[:, core] = mine_ref[...]
    rows_ref[:, 1 - core] = other_ref[...]
    out_ref[...] = dot_nt(cot_ref[...], rows_ref[...].reshape(4 * HEAD_DIM, WIDTH)).astype(jnp.bfloat16)


def grad_attention(far, place, cot, mine, other):
    piece = pl.BlockSpec((2, HEAD_DIM, WIDTH), lambda i, *_: (i, 0, 0))
    return pl.pallas_call(
        grad_attn_kernel,
        grid_spec=pltpu.PrefetchScalarGridSpec(
            num_scalar_prefetch=1,
            grid=(2,),
            in_specs=[fixed((TOK, WIDTH)), piece, piece],
            out_specs=pl.BlockSpec((TOK, 4 * HEAD_DIM), lambda i, *_: (0, i)),
            scratch_shapes=[pltpu.VMEM((2, 2, HEAD_DIM, WIDTH), jnp.bfloat16)],
        ),
        out_shape=jax.ShapeDtypeStruct((TOK, WIDTH // 2), jnp.bfloat16),
        compiler_params=params(),
        cost_estimate=cost(7e9),
        name="grad_far" if far else "grad_near",
    )(place, cot, mine, other)


def place_weights(place_ref, refs, rows_ref):
    core = place_ref[0]
    zh = place_ref[1]
    near_ref, far_ref, near_other_ref, far_other_ref = refs
    rows_ref[:, zh, core] = near_ref[...]
    rows_ref[:, 1 - zh, core] = far_ref[...]
    rows_ref[:, zh, 1 - core] = near_other_ref[...]
    rows_ref[:, 1 - zh, 1 - core] = far_other_ref[...]


def project_kernel(place_ref, early_ref, late_ref, *refs):
    *weights, out_ref, rows_ref = refs
    place_weights(place_ref, weights, rows_ref)
    weight = rows_ref[...].reshape(WIDTH, out_ref.shape[1])
    out_ref[:BLOCK] = dot_nn(early_ref[...], weight).astype(jnp.bfloat16)
    out_ref[BLOCK:] = dot_nn(late_ref[...], weight).astype(jnp.bfloat16)


def project(place, early, late, *weights):
    tile = 512
    piece = pl.BlockSpec((4, HEAD_DIM, tile), lambda i, *_: (0, 0, i))
    return pl.pallas_call(
        project_kernel,
        grid_spec=pltpu.PrefetchScalarGridSpec(
            num_scalar_prefetch=1,
            grid=(WIDTH // tile,),
            in_specs=[fixed((BLOCK, WIDTH)), fixed((BLOCK, WIDTH))] + [piece] * 4,
            out_specs=pl.BlockSpec((TOK, tile), lambda i, *_: (0, i)),
            scratch_shapes=[pltpu.VMEM((4, 2, 2, HEAD_DIM, tile), jnp.bfloat16)],
        ),
        out_shape=jax.ShapeDtypeStruct((TOK, WIDTH), jnp.bfloat16),
        compiler_params=params(),
        cost_estimate=cost(8e9),
        name="project",
    )(place, early, late, *weights)


def sum_pieces_kernel(pieces_ref, out_ref):
    total = pieces_ref[0].astype(jnp.float32)
    for i in range(1, pieces_ref.shape[0]):
        total += pieces_ref[i].astype(jnp.float32)
    total = total.astype(jnp.bfloat16)
    for i in range(out_ref.shape[0]):
        out_ref[i] = total


def sum_pieces(pieces, copies):
    count, rows, width = pieces.shape
    tile = 512
    return pl.pallas_call(
        sum_pieces_kernel,
        grid=(width // tile,),
        in_specs=[pl.BlockSpec((count, rows, tile), lambda i: (0, 0, i))],
        out_specs=pl.BlockSpec((copies, rows, tile), lambda i: (0, 0, i)),
        out_shape=jax.ShapeDtypeStruct((copies, rows, width), jnp.bfloat16),
        compiler_params=params(),
        cost_estimate=cost(2e9),
        name="sum_pieces",
    )(pieces)


def swapped(array):
    return lax.ppermute(array, "core", [(0, 1), (1, 0)])


def passed_along(array, by):
    devices = 16
    pairs = [(i, i + by) for i in range(devices) if 0 <= i + by < devices]
    return lax.ppermute(array, GROUP_AXES, pairs)


def across_z(array):
    return lax.ppermute(array, ("zh", "zl"), [(z, 3 - z) for z in range(4)])


def tied(array, *others):
    return lax.optimization_barrier((array, *others))[0]


def on_device(query_rows, key_rows, value_rows, pyramid_start, scale_end, out_weight, cotangent):
    core = lax.axis_index("core").astype(jnp.int32)
    group_index = lax.axis_index(GROUP_AXES).astype(jnp.int32)
    core_arg = core.reshape(1)
    place = jnp.stack([core, lax.axis_index("zh").astype(jnp.int32)])
    start = (pyramid_start - group_index * TOK).reshape(1, TOK)
    end = (scale_end - group_index * TOK).reshape(1, TOK)

    after_rows = jnp.concatenate([key_rows[:AFTER], value_rows[:AFTER]], axis=1)
    after = passed_along(after_rows, -1)
    half = lax.dynamic_slice_in_dim(tied(out_weight, after_rows), core * HEAD_DIM, HEAD_DIM, 0)
    far_half = across_z(half)
    near_halves = jnp.broadcast_to(half, (4, HEAD_DIM, WIDTH))
    near = lax.all_to_all(near_halves, "y", 0, 0, tiled=True)
    before_rows = jnp.concatenate([key_rows[TOK - BEFORE:], value_rows[TOK - BEFORE:]], axis=1)
    before_rows = tied(before_rows, near_halves, after)
    before = passed_along(before_rows, 1)
    cot_peer = swapped(tied(cotangent, half))

    late, late_theirs, late_lse = forward(True, core_arg, start, end, tied(query_rows, far_half), key_rows, value_rows, after)
    far_half = tied(far_half, near, late)
    far = lax.all_to_all(jnp.broadcast_to(far_half, (4, HEAD_DIM, WIDTH)), "y", 0, 0, tiled=True)
    peer_late = swapped(late_theirs)
    early, early_theirs, early_lse = forward(False, core_arg, start, end, query_rows, key_rows, value_rows, before)
    peer_early = swapped(early_theirs)
    near_other = swapped(tied(near, late))
    sums = weight_sums(core_arg, early, late, peer_early, peer_late, cotangent, tied(cot_peer, near_other))
    grad_near = grad_attention(False, place, tied(cotangent, sums), near, near_other)
    far = tied(far, grad_near)
    sums = tied(sums.reshape(4, 2 * HEAD_DIM, WIDTH), far)
    pieces = lax.all_to_all(sums, "y", 0, 0, tiled=True)

    far_other = swapped(far)
    grad_far = grad_attention(True, place, cotangent, far, far_other)
    weights = (near, far, near_other, far_other)
    dq, dk0, dv0, halo = backward(
        False, place, start, end, early_lse, query_rows, grad_near, grad_far, key_rows, value_rows, before)
    from_next = passed_along(halo, -1)
    dq, dk1, dv1, halo = backward(
        True, place, start, end, late_lse, query_rows, grad_near, grad_far, key_rows, value_rows, after, dk0, dv0, dq)
    from_prev = passed_along(halo, 1)

    layer_out = project(place, tied(early, dk1), late, *weights)
    partial = sum_pieces(tied(pieces, layer_out), 1).reshape(16, 16, WIDTH)
    shares = lax.all_to_all(partial, ("zh", "x", "zl"), 0, 0, tiled=True)
    key_grad, value_grad = finish(tied(dk1, partial), dv1, from_next, from_prev)
    summed = sum_pieces(tied(shares, key_grad), 8)
    rows_mine = lax.all_to_all(summed, ("x", "zl"), 0, 0, tiled=True).reshape(HEAD_DIM, WIDTH)
    rows_other = swapped(rows_mine)
    first = jnp.where(core == 0, rows_mine, rows_other)
    second = jnp.where(core == 0, rows_other, rows_mine)
    weight_grad = jnp.concatenate([first, second], axis=0).astype(jnp.float32) * (float(TOKENS) ** -0.5)
    return (layer_out, dq, key_grad, value_grad, weight_grad)


def solution(mesh):
    inner = Mesh(mesh.devices.reshape(SIZES), AXES)
    rows = P(AXES, None)
    shard = P(("y", "zh"), None)
    return jax.shard_map(
        on_device,
        mesh=inner,
        in_specs=(rows, rows, rows, P(AXES), P(AXES), shard, rows),
        out_specs=(rows, rows, rows, rows, shard),
        check_vma=False,
    )
```

```python
import functools

import jax
import jax.numpy as jnp
from jax import lax
from jax.experimental import pallas as pl
from jax.experimental.pallas import tpu as pltpu
from jax.sharding import Mesh, PartitionSpec as P

HEADS = 16
HEAD_DIM = 128
WIDTH = HEADS * HEAD_DIM
TOK = 512
BLOCK = 256
BEFORE = 256
AFTER = 128
SENT_AFTER = 112
SPAN = 640
FACTOR = HEAD_DIM ** -0.5
TOKENS = 65536

AXES = ("y", "zh", "x", "zl", "core")
SIZES = (4, 2, 4, 2, 2)
GROUP_AXES = ("x", "zl", "core")
MB = 1024 * 1024
PER_STEP = 4
STEPS = HEADS // PER_STEP
COLS = PER_STEP * HEAD_DIM


def dot_nt(left, right):
    return lax.dot_general(left, right, (((1,), (1,)), ((), ())), preferred_element_type=jnp.float32)


def dot_nn(left, right):
    return lax.dot_general(left, right, (((1,), (0,)), ((), ())), preferred_element_type=jnp.float32)


def dot_tn(left, right):
    return lax.dot_general(left, right, (((0,), (0,)), ((), ())), preferred_element_type=jnp.float32)


def fixed(shape):
    return pl.BlockSpec(shape, lambda i, *_: (0,) * len(shape))


def columns(rows, shift=0, row_block=0):
    return pl.BlockSpec((rows, COLS), lambda i, *_: (row_block, i + shift))


def halo_columns(rows):
    return pl.BlockSpec((2, rows, COLS), lambda i, *_: (0, 0, i))


def cost(flops):
    return pl.CostEstimate(flops=int(flops * 1e-3), bytes_accessed=0, transcendentals=0)


def params():
    return pltpu.CompilerParams(vmem_limit_bytes=56 * MB)


def fill_bias(late, start_ref, end_ref, bias_ref):
    first = 0 if late else -BEFORE
    pos = lax.broadcasted_iota(jnp.int32, (SPAN, BLOCK), 0) + first
    ok = (pos >= start_ref[...]) & (pos < end_ref[...])
    bias_ref[...] = jnp.where(ok, 0.0, -jnp.inf).astype(jnp.float32)


def gather_keys(late, own, halo):
    if late:
        return jnp.concatenate([own, halo], axis=0)
    return jnp.concatenate([halo, own[: SPAN - BEFORE]], axis=0)


HALVES = ((slice(0, 128), slice(0, 512)), (slice(128, 256), slice(128, 640)))


def assemble(first, second):
    none = jnp.zeros((SPAN - 512, 128), first.dtype)
    return jnp.concatenate([jnp.concatenate([first, none], axis=0), jnp.concatenate([none, second], axis=0)], axis=1)


def forward_kernel(core_ref, start_ref, end_ref, q_ref, ko_ref, kh_ref, vo_ref, vh_ref,
                   out_ref, theirs_ref, lse_ref, bias_ref, *, late):
    @pl.when(pl.program_id(0) == 0)
    def _():
        fill_bias(late, start_ref, end_ref, bias_ref)

    even = core_ref[0] == 0
    outs = []

    def head(h):
        return slice(h * HEAD_DIM, (h + 1) * HEAD_DIM)

    def scores(h):
        return dot_nt(gather_keys(late, ko_ref[:, head(h)], kh_ref[:, head(h)]), q_ref[:, head(h)])

    def weigh(s):
        parts = []
        for queries, keys in HALVES:
            part = s[keys, queries] + bias_ref[keys, queries]
            top = jnp.max(part, axis=0, keepdims=True)
            e = jnp.exp((part - top) * FACTOR)
            total = jnp.sum(e, axis=0, keepdims=True)
            parts.append((e.astype(jnp.bfloat16), top, total))
        first, second = parts
        return (assemble(first[0], second[0]), jnp.concatenate([first[1], second[1]], axis=1),
                jnp.concatenate([first[2], second[2]], axis=1))

    def mix(h, e, top, total):
        v = gather_keys(late, vo_ref[:, head(h)], vh_ref[:, head(h)])
        out = (dot_nn(v.T, e) * (1.0 / total)).T.astype(jnp.bfloat16)
        out_ref[:, head(h)] = out
        lse_ref[h] = top * FACTOR + jnp.log(total)
        outs.append(out)
        if h % 2:
            theirs_ref[:, head(h // 2)] = jnp.where(even, outs[h], outs[h - 1])

    ahead = scores(0)
    behind = None
    for h in range(PER_STEP):
        now, ahead = ahead, scores(h + 1) if h + 1 < PER_STEP else None
        weighed = weigh(now)
        if behind is not None:
            mix(h - 1, *behind)
        behind = weighed
    mix(PER_STEP - 1, *behind)


def forward(late, core, start, end, q, k, v, halo):
    row_block = 1 if late else 0
    halo_rows = AFTER if late else BEFORE
    bounds = pl.BlockSpec((1, BLOCK), lambda i, *_: (0, row_block))
    return pl.pallas_call(
        functools.partial(forward_kernel, late=late),
        grid_spec=pltpu.PrefetchScalarGridSpec(
            num_scalar_prefetch=1,
            grid=(STEPS,),
            in_specs=[bounds, bounds, columns(BLOCK, row_block=row_block),
                      columns(TOK), columns(halo_rows), columns(TOK), columns(halo_rows, STEPS)],
            out_specs=[columns(BLOCK),
                       pl.BlockSpec((BLOCK, COLS // 2), lambda i, *_: (0, i)),
                       pl.BlockSpec((PER_STEP, 1, BLOCK), lambda i, *_: (i, 0, 0))],
            scratch_shapes=[pltpu.VMEM((SPAN, BLOCK), jnp.float32)],
        ),
        out_shape=[jax.ShapeDtypeStruct((BLOCK, WIDTH), jnp.bfloat16),
                   jax.ShapeDtypeStruct((BLOCK, WIDTH // 2), jnp.bfloat16),
                   jax.ShapeDtypeStruct((HEADS, 1, BLOCK), jnp.float32)],
        compiler_params=params(),
        cost_estimate=cost(8e9),
        name="attend_late" if late else "attend_early",
    )(core, start, end, q, k, halo, v, halo)


def backward_kernel(start_ref, end_ref, lse_early_ref, lse_late_ref, q_ref, g_ref, ko_ref, kb_ref, ka_ref,
                    vo_ref, vb_ref, va_ref, *refs):
    dq_ref, dk_ref, dv_ref, before_ref, after_ref, bias_ref = refs[-6:]

    @pl.when(pl.program_id(0) == 0)
    def _():
        for late in (False, True):
            block = slice(BLOCK, 2 * BLOCK) if late else slice(0, BLOCK)
            fill_bias(late, start_ref.at[:, block], end_ref.at[:, block], bias_ref.at[int(late)])

    def head(h):
        return slice(h * HEAD_DIM, (h + 1) * HEAD_DIM)

    def products(h, late):
        cols = head(h)
        halves = (ka_ref, va_ref) if late else (kb_ref, vb_ref)
        k = gather_keys(late, ko_ref[:, cols], halves[0][:, cols])
        v = gather_keys(late, vo_ref[:, cols], halves[1][:, cols])
        q = q_ref[late * BLOCK:(late + 1) * BLOCK, cols]
        g = g_ref[late * BLOCK:(late + 1) * BLOCK, cols]
        return k, q, g, [(dot_nt(k[keys], q[queries]), dot_nt(v[keys], g[queries])) for queries, keys in HALVES]

    def differentiate(h, late, k, q, g, pairs):
        lse_ref = lse_late_ref if late else lse_early_ref
        probs = []
        grads = []
        for (queries, keys), (s, dp) in zip(HALVES, pairs):
            p = jnp.exp((s + bias_ref[late, keys, queries]) * FACTOR - lse_ref[h, :, queries])
            inner = jnp.sum(p * dp, axis=0, keepdims=True)
            probs.append(p.astype(jnp.bfloat16))
            grads.append((p * (dp - inner)).astype(jnp.bfloat16))
        return k, q, g, assemble(*probs), assemble(*grads)

    early = {}

    def collect(h, late, k, q, g, p, ds):
        cols = head(h)
        dv = dot_nn(p, g)
        dk = dot_nn(ds, q) * FACTOR
        dq_ref[late * BLOCK:(late + 1) * BLOCK, cols] = (dot_nn(k.T, ds) * FACTOR).T.astype(jnp.bfloat16)
        if not late:
            early[h] = dk, dv
            before_ref[0, :, cols] = dk[:BEFORE].astype(jnp.bfloat16)
            before_ref[1, :, cols] = dv[:BEFORE].astype(jnp.bfloat16)
            return
        keep = SPAN - BEFORE
        for out_ref, first, second, i in ((dk_ref, early[h][0], dk, 0), (dv_ref, early[h][1], dv, 1)):
            out_ref[:keep, cols] = (first[BEFORE:] + second[:keep]).astype(jnp.bfloat16)
            out_ref[keep:, cols] = second[keep:TOK].astype(jnp.bfloat16)
            after_ref[i, :, cols] = second[TOK:TOK + SENT_AFTER].astype(jnp.bfloat16)

    units = [(h, late) for h in range(PER_STEP) for late in (0, 1)]
    ahead = products(*units[0])
    behind = None
    for i, unit in enumerate(units):
        now, ahead = ahead, products(*units[i + 1]) if i + 1 < len(units) else None
        done = differentiate(*unit, *now)
        if behind is not None:
            collect(*units[i - 1], *behind)
        behind = done
    collect(*units[-1], *behind)


def backward(half, start, end, lse_early, lse_late, q, g, k, v, before, after, *earlier):
    shape = jax.ShapeDtypeStruct
    steps = STEPS // 2
    first = half * steps
    lse = pl.BlockSpec((PER_STEP, 1, BLOCK), lambda i: (i + first, 0, 0))
    own = columns(TOK, first)
    return pl.pallas_call(
        backward_kernel,
        grid=(steps,),
        in_specs=[fixed((1, TOK)), fixed((1, TOK)), lse, lse, own, own,
                  own, columns(BEFORE, first), columns(AFTER, first),
                  own, columns(BEFORE, STEPS + first), columns(AFTER, STEPS + first)]
        + [pl.BlockSpec(memory_space=pl.ANY)] * len(earlier),
        out_specs=[own, own, own, halo_columns(BEFORE), halo_columns(SENT_AFTER)],
        out_shape=[shape((TOK, WIDTH), jnp.bfloat16)] * 3
        + [shape((2, BEFORE, WIDTH // 2), jnp.bfloat16), shape((2, SENT_AFTER, WIDTH // 2), jnp.bfloat16)],
        input_output_aliases={12 + i: i for i in range(len(earlier))},
        scratch_shapes=[pltpu.VMEM((2, SPAN, BLOCK), jnp.float32)],
        compiler_params=params(),
        cost_estimate=cost(10e9),
        name="attend_backward_second" if half else "attend_backward_first",
    )(start, end, lse_early, lse_late, q, g, k, before, after, v, before, after, *earlier)


def finish_kernel(dk_ref, dv_ref, first_ref, second_ref, dk_out_ref, dv_out_ref):
    def add(halo_ref):
        for i, own_ref, out_ref in ((0, dk_ref, dk_out_ref), (1, dv_ref, dv_out_ref)):
            total = own_ref[...].astype(jnp.float32) + halo_ref[i].astype(jnp.float32)
            out_ref[...] = total.astype(jnp.bfloat16)

    step = pl.program_id(0)
    pl.when(step < STEPS // 2)(lambda: add(first_ref))
    pl.when(step >= STEPS // 2)(lambda: add(second_ref))


def finish(dk, dv, first, second):
    rows = first.shape[1]
    half = STEPS // 2
    part = columns(rows, row_block=(TOK - rows) // rows if rows == BEFORE else 0)
    return pl.pallas_call(
        finish_kernel,
        grid=(STEPS,),
        in_specs=[part, part,
                  pl.BlockSpec((2, rows, COLS), lambda i: (0, 0, jnp.minimum(i, half - 1))),
                  pl.BlockSpec((2, rows, COLS), lambda i: (0, 0, jnp.maximum(i - half, 0)))],
        out_specs=[part, part],
        out_shape=[jax.ShapeDtypeStruct((TOK, WIDTH), jnp.bfloat16)] * 2,
        input_output_aliases={0: 0, 1: 1},
        compiler_params=params(),
        cost_estimate=cost(2e9),
        name="finish_grads",
    )(dk, dv, first, second)


def weight_sums_kernel(core_ref, early_ref, late_ref, peer_early_ref, peer_late_ref, cot_ref, cot_peer_ref, out_ref):
    own = jnp.concatenate([early_ref[...], late_ref[...]], axis=0)
    peer = jnp.concatenate([peer_early_ref[...], peer_late_ref[...]], axis=0)
    core = core_ref[0]
    parts = [jnp.where(core == 0, own[:, 2 * j * HEAD_DIM:(2 * j + 1) * HEAD_DIM],
                       own[:, (2 * j + 1) * HEAD_DIM:(2 * j + 2) * HEAD_DIM]) for j in range(4)]
    own = jnp.concatenate(parts, axis=1)
    out_ref[...] = (dot_tn(own, cot_ref[...]) + dot_tn(peer, cot_peer_ref[...])).astype(jnp.bfloat16)


def weight_sums(core, early, late, peer_early, peer_late, cot, cot_peer):
    own_spec = pl.BlockSpec((BLOCK, 8 * HEAD_DIM), lambda i, *_: (0, i))
    peer_spec = pl.BlockSpec((BLOCK, 4 * HEAD_DIM), lambda i, *_: (0, i))
    return pl.pallas_call(
        weight_sums_kernel,
        grid_spec=pltpu.PrefetchScalarGridSpec(
            num_scalar_prefetch=1,
            grid=(2,),
            in_specs=[own_spec, own_spec, peer_spec, peer_spec, fixed((TOK, WIDTH)), fixed((TOK, WIDTH))],
            out_specs=pl.BlockSpec((4 * HEAD_DIM, WIDTH), lambda i, *_: (i, 0)),
        ),
        out_shape=jax.ShapeDtypeStruct((WIDTH // 2, WIDTH), jnp.bfloat16),
        compiler_params=params(),
        cost_estimate=cost(7e9),
        name="weight_sums",
    )(core, early, late, peer_early, peer_late, cot, cot_peer)


def place_weights(place_ref, refs, rows_ref):
    core = place_ref[0]
    zh = place_ref[1]
    near_ref, far_ref, near_other_ref, far_other_ref = refs
    rows_ref[:, zh, core] = near_ref[...]
    rows_ref[:, 1 - zh, core] = far_ref[...]
    rows_ref[:, zh, 1 - core] = near_other_ref[...]
    rows_ref[:, 1 - zh, 1 - core] = far_other_ref[...]


def grad_attn_kernel(place_ref, cot_ref, *refs):
    *weights, out_ref, rows_ref = refs
    place_weights(place_ref, weights, rows_ref)
    out_ref[...] = dot_nt(cot_ref[...], rows_ref[...].reshape(4 * HEAD_DIM, WIDTH)).astype(jnp.bfloat16)


def grad_attention(place, cot, *weights):
    piece = pl.BlockSpec((1, HEAD_DIM, WIDTH), lambda i, *_: (i, 0, 0))
    return pl.pallas_call(
        grad_attn_kernel,
        grid_spec=pltpu.PrefetchScalarGridSpec(
            num_scalar_prefetch=1,
            grid=(4,),
            in_specs=[fixed((TOK, WIDTH))] + [piece] * 4,
            out_specs=pl.BlockSpec((TOK, 4 * HEAD_DIM), lambda i, *_: (0, i)),
            scratch_shapes=[pltpu.VMEM((1, 2, 2, HEAD_DIM, WIDTH), jnp.bfloat16)],
        ),
        out_shape=jax.ShapeDtypeStruct((TOK, WIDTH), jnp.bfloat16),
        compiler_params=params(),
        cost_estimate=cost(7e9),
        name="grad_attention",
    )(place, cot, *weights)


def project_kernel(place_ref, early_ref, late_ref, *refs):
    *weights, out_ref, rows_ref, attn_ref = refs

    @pl.when(pl.program_id(0) == 0)
    def _():
        attn_ref[:BLOCK] = early_ref[...]
        attn_ref[BLOCK:] = late_ref[...]

    place_weights(place_ref, weights, rows_ref)
    out_ref[...] = dot_nn(attn_ref[...], rows_ref[...].reshape(WIDTH, out_ref.shape[1])).astype(jnp.bfloat16)


def project(place, early, late, *weights):
    tile = 512
    piece = pl.BlockSpec((4, HEAD_DIM, tile), lambda i, *_: (0, 0, i))
    return pl.pallas_call(
        project_kernel,
        grid_spec=pltpu.PrefetchScalarGridSpec(
            num_scalar_prefetch=1,
            grid=(WIDTH // tile,),
            in_specs=[fixed((BLOCK, WIDTH)), fixed((BLOCK, WIDTH))] + [piece] * 4,
            out_specs=pl.BlockSpec((TOK, tile), lambda i, *_: (0, i)),
            scratch_shapes=[pltpu.VMEM((4, 2, 2, HEAD_DIM, tile), jnp.bfloat16), pltpu.VMEM((TOK, WIDTH), jnp.bfloat16)],
        ),
        out_shape=jax.ShapeDtypeStruct((TOK, WIDTH), jnp.bfloat16),
        compiler_params=params(),
        cost_estimate=cost(8e9),
        name="project",
    )(place, early, late, *weights)


def sum_pieces_kernel(pieces_ref, out_ref):
    total = pieces_ref[0].astype(jnp.float32)
    for i in range(1, pieces_ref.shape[0]):
        total += pieces_ref[i].astype(jnp.float32)
    total = total.astype(jnp.bfloat16)
    for i in range(out_ref.shape[0]):
        out_ref[i] = total


def sum_pieces(pieces, copies, tile):
    count, rows, width = pieces.shape
    return pl.pallas_call(
        sum_pieces_kernel,
        grid=(rows // tile,),
        in_specs=[pl.BlockSpec((count, tile, width), lambda i: (0, i, 0))],
        out_specs=pl.BlockSpec((copies, tile, width), lambda i: (0, i, 0)),
        out_shape=jax.ShapeDtypeStruct((copies, rows, width), jnp.bfloat16),
        compiler_params=params(),
        cost_estimate=cost(2e9),
        name="sum_pieces",
    )(pieces)


def swapped(array):
    return lax.ppermute(array, "core", [(0, 1), (1, 0)])


def passed_along(array, by):
    devices = 16
    pairs = [(i, i + by) for i in range(devices) if 0 <= i + by < devices]
    return lax.ppermute(array, GROUP_AXES, pairs)


def across_z(array):
    return lax.ppermute(array, ("zh", "zl"), [(z, 3 - z) for z in range(4)])


def tied(array, *others):
    return lax.optimization_barrier((array, *others))[0]


def on_device(query_rows, key_rows, value_rows, pyramid_start, scale_end, out_weight, cotangent):
    core = lax.axis_index("core").astype(jnp.int32)
    group_index = lax.axis_index(GROUP_AXES).astype(jnp.int32)
    core_arg = core.reshape(1)
    place = jnp.stack([core, lax.axis_index("zh").astype(jnp.int32)])
    start = (pyramid_start - group_index * TOK).reshape(1, TOK)
    end = (scale_end - group_index * TOK).reshape(1, TOK)

    half = lax.dynamic_slice_in_dim(out_weight, core * HEAD_DIM, HEAD_DIM, 0)
    near_halves = jnp.broadcast_to(half, (4, HEAD_DIM, WIDTH))
    near = lax.all_to_all(near_halves, "y", 0, 0, tiled=True)
    far_half = across_z(half)
    after_rows = jnp.concatenate([key_rows[:AFTER], value_rows[:AFTER]], axis=1)
    after_rows = tied(after_rows, near_halves)
    after = passed_along(after_rows, -1)
    before_rows = jnp.concatenate([key_rows[TOK - BEFORE:], value_rows[TOK - BEFORE:]], axis=1)
    before = passed_along(tied(before_rows, after_rows, after), 1)
    cot_peer = swapped(tied(cotangent, after_rows))
    far_halves = jnp.broadcast_to(far_half, (4, HEAD_DIM, WIDTH))

    late, late_theirs, late_lse = forward(
        True, core_arg, start, end, tied(query_rows, far_halves), key_rows, value_rows, after)
    far = lax.all_to_all(tied(far_halves, near, late), "y", 0, 0, tiled=True)
    peer_late = swapped(late_theirs)
    early, early_theirs, early_lse = forward(
        False, core_arg, start, end, tied(query_rows, peer_late), key_rows, value_rows, before)
    peer_early = swapped(early_theirs)
    near_other = swapped(tied(near, late))
    sums = weight_sums(core_arg, early, late, peer_early, peer_late, cotangent, tied(cot_peer, near_other))
    far = tied(far, sums)
    pieces = lax.all_to_all(tied(sums.reshape(4, 2 * HEAD_DIM, WIDTH), far), "y", 0, 0, tiled=True)
    far_other = swapped(far)
    weights = (near, far, near_other, far_other)
    grad_attn = grad_attention(place, tied(cotangent, far), *weights)
    shared = (start, end, early_lse, late_lse, query_rows, grad_attn, key_rows, value_rows, before, after)
    dq, dk, dv, to_previous, to_next = backward(0, *shared)
    from_next = [passed_along(to_previous, -1)]
    from_prev = [passed_along(to_next, 1)]
    dq, dk, dv, to_previous, to_next = backward(1, *shared, dq, dk, dv)
    from_next.append(passed_along(to_previous, -1))
    from_prev.append(passed_along(to_next, 1))

    partial = tied(sum_pieces(tied(pieces, dk), 1, 128), from_prev[0], from_next[0]).reshape(16, 16, WIDTH)
    shares = lax.all_to_all(partial, ("zh", "x", "zl"), 0, 0, tiled=True)
    layer_out = project(place, tied(early, partial, from_next[1]), late, *weights)
    summed = sum_pieces(tied(shares, layer_out), 8, 16)
    rows_mine = lax.all_to_all(summed, ("x", "zl"), 0, 0, tiled=True).reshape(HEAD_DIM, WIDTH)
    dk, dv = finish(tied(dk, summed), dv, *from_prev)
    key_grad, value_grad = finish(dk, dv, *from_next)
    rows_mine = tied(rows_mine, key_grad)
    rows_other = swapped(rows_mine)
    first = jnp.where(core == 0, rows_mine, rows_other)
    second = jnp.where(core == 0, rows_other, rows_mine)
    weight_grad = jnp.concatenate([first, second], axis=0).astype(jnp.float32) * (float(TOKENS) ** -0.5)
    return (layer_out, dq, key_grad, value_grad, weight_grad)


def solution(mesh):
    inner = Mesh(mesh.devices.reshape(SIZES), AXES)
    rows = P(AXES, None)
    shard = P(("y", "zh"), None)
    return jax.shard_map(
        on_device,
        mesh=inner,
        in_specs=(rows, rows, rows, P(AXES), P(AXES), shard, rows),
        out_specs=(rows, rows, rows, rows, shard),
        check_vma=False,
    )
```

```python
import functools

import jax
import jax.numpy as jnp
from jax import lax
from jax.experimental import pallas as pl
from jax.experimental.pallas import tpu as pltpu
from jax.sharding import Mesh, PartitionSpec as P

HEADS = 16
HEAD_DIM = 128
WIDTH = HEADS * HEAD_DIM
TOK = 512
BLOCK = 256
BEFORE = 256
AFTER = 128
SENT_AFTER = 112
SPAN = 640
FACTOR = HEAD_DIM ** -0.5
TOKENS = 65536

AXES = ("y", "zh", "x", "zl", "core")
SIZES = (4, 2, 4, 2, 2)
GROUP_AXES = ("x", "zl", "core")
MB = 1024 * 1024
PER_STEP = 4
STEPS = HEADS // PER_STEP
COLS = PER_STEP * HEAD_DIM


def dot_nt(left, right):
    return lax.dot_general(left, right, (((1,), (1,)), ((), ())), preferred_element_type=jnp.float32)


def dot_nn(left, right):
    return lax.dot_general(left, right, (((1,), (0,)), ((), ())), preferred_element_type=jnp.float32)


def dot_tn(left, right):
    return lax.dot_general(left, right, (((0,), (0,)), ((), ())), preferred_element_type=jnp.float32)


def fixed(shape):
    return pl.BlockSpec(shape, lambda i, *_: (0,) * len(shape))


def columns(rows, shift=0, row_block=0):
    return pl.BlockSpec((rows, COLS), lambda i, *_: (row_block, i + shift))


def halo_columns(rows):
    return pl.BlockSpec((2, rows, COLS), lambda i, *_: (0, 0, i))


def cost(flops):
    return pl.CostEstimate(flops=int(flops * 1e-3), bytes_accessed=0, transcendentals=0)


def params():
    return pltpu.CompilerParams(vmem_limit_bytes=56 * MB)


def fill_bias(late, start_ref, end_ref, bias_ref):
    first = 0 if late else -BEFORE
    pos = lax.broadcasted_iota(jnp.int32, (SPAN, BLOCK), 0) + first
    ok = (pos >= start_ref[...]) & (pos < end_ref[...])
    bias_ref[...] = jnp.where(ok, 0.0, -jnp.inf).astype(jnp.float32)


def gather_keys(late, own, halo):
    if late:
        return jnp.concatenate([own, halo], axis=0)
    return jnp.concatenate([halo, own[: SPAN - BEFORE]], axis=0)


HALVES = ((slice(0, 128), slice(0, 512)), (slice(128, 256), slice(128, 640)))


def assemble(first, second):
    none = jnp.zeros((SPAN - 512, 128), first.dtype)
    return jnp.concatenate([jnp.concatenate([first, none], axis=0), jnp.concatenate([none, second], axis=0)], axis=1)


def forward_kernel(core_ref, start_ref, end_ref, q_ref, ko_ref, kh_ref, vo_ref, vh_ref,
                   out_ref, theirs_ref, lse_ref, bias_ref, *, late):
    @pl.when(pl.program_id(0) == 0)
    def _():
        fill_bias(late, start_ref, end_ref, bias_ref)

    even = core_ref[0] == 0
    outs = []

    def head(h):
        return slice(h * HEAD_DIM, (h + 1) * HEAD_DIM)

    def scores(h):
        return dot_nt(gather_keys(late, ko_ref[:, head(h)], kh_ref[:, head(h)]), q_ref[:, head(h)])

    def weigh(s):
        parts = []
        for queries, keys in HALVES:
            part = s[keys, queries] + bias_ref[keys, queries]
            top = jnp.max(part, axis=0, keepdims=True)
            e = jnp.exp((part - top) * FACTOR)
            total = jnp.sum(e, axis=0, keepdims=True)
            parts.append((e.astype(jnp.bfloat16), top, total))
        first, second = parts
        return (assemble(first[0], second[0]), jnp.concatenate([first[1], second[1]], axis=1),
                jnp.concatenate([first[2], second[2]], axis=1))

    def mix(h, e, top, total):
        v = gather_keys(late, vo_ref[:, head(h)], vh_ref[:, head(h)])
        out = (dot_nn(v.T, e) * (1.0 / total)).T.astype(jnp.bfloat16)
        out_ref[:, head(h)] = out
        lse_ref[h] = top * FACTOR + jnp.log(total)
        outs.append(out)
        if h % 2:
            theirs_ref[:, head(h // 2)] = jnp.where(even, outs[h], outs[h - 1])

    ahead = scores(0)
    behind = None
    for h in range(PER_STEP):
        now, ahead = ahead, scores(h + 1) if h + 1 < PER_STEP else None
        weighed = weigh(now)
        if behind is not None:
            mix(h - 1, *behind)
        behind = weighed
    mix(PER_STEP - 1, *behind)


def forward(late, core, start, end, q, k, v, halo):
    row_block = 1 if late else 0
    halo_rows = AFTER if late else BEFORE
    bounds = pl.BlockSpec((1, BLOCK), lambda i, *_: (0, row_block))
    return pl.pallas_call(
        functools.partial(forward_kernel, late=late),
        grid_spec=pltpu.PrefetchScalarGridSpec(
            num_scalar_prefetch=1,
            grid=(STEPS,),
            in_specs=[bounds, bounds, columns(BLOCK, row_block=row_block),
                      columns(TOK), columns(halo_rows), columns(TOK), columns(halo_rows, STEPS)],
            out_specs=[columns(BLOCK),
                       pl.BlockSpec((BLOCK, COLS // 2), lambda i, *_: (0, i)),
                       pl.BlockSpec((PER_STEP, 1, BLOCK), lambda i, *_: (i, 0, 0))],
            scratch_shapes=[pltpu.VMEM((SPAN, BLOCK), jnp.float32)],
        ),
        out_shape=[jax.ShapeDtypeStruct((BLOCK, WIDTH), jnp.bfloat16),
                   jax.ShapeDtypeStruct((BLOCK, WIDTH // 2), jnp.bfloat16),
                   jax.ShapeDtypeStruct((HEADS, 1, BLOCK), jnp.float32)],
        compiler_params=params(),
        cost_estimate=cost(8e9),
        name="attend_late" if late else "attend_early",
    )(core, start, end, q, k, halo, v, halo)


def backward_kernel(start_ref, end_ref, lse_early_ref, lse_late_ref, q_ref, g_ref, ko_ref, kb_ref, ka_ref,
                    vo_ref, vb_ref, va_ref, *refs):
    dq_ref, dk_ref, dv_ref, before_ref, after_ref, bias_ref = refs[-6:]

    @pl.when(pl.program_id(0) == 0)
    def _():
        for late in (False, True):
            block = slice(BLOCK, 2 * BLOCK) if late else slice(0, BLOCK)
            fill_bias(late, start_ref.at[:, block], end_ref.at[:, block], bias_ref.at[int(late)])

    def head(h):
        return slice(h * HEAD_DIM, (h + 1) * HEAD_DIM)

    def products(h, late):
        cols = head(h)
        halves = (ka_ref, va_ref) if late else (kb_ref, vb_ref)
        k = gather_keys(late, ko_ref[:, cols], halves[0][:, cols])
        v = gather_keys(late, vo_ref[:, cols], halves[1][:, cols])
        q = q_ref[late * BLOCK:(late + 1) * BLOCK, cols]
        g = g_ref[late * BLOCK:(late + 1) * BLOCK, cols]
        return k, q, g, [(dot_nt(k[keys], q[queries]), dot_nt(v[keys], g[queries])) for queries, keys in HALVES]

    def differentiate(h, late, k, q, g, pairs):
        lse_ref = lse_late_ref if late else lse_early_ref
        probs = []
        grads = []
        for (queries, keys), (s, dp) in zip(HALVES, pairs):
            p = jnp.exp((s + bias_ref[late, keys, queries]) * FACTOR - lse_ref[h, :, queries])
            inner = jnp.sum(p * dp, axis=0, keepdims=True)
            probs.append(p.astype(jnp.bfloat16))
            grads.append((p * (dp - inner)).astype(jnp.bfloat16))
        return k, q, g, assemble(*probs), assemble(*grads)

    early = {}

    def collect(h, late, k, q, g, p, ds):
        cols = head(h)
        dv = dot_nn(p, g)
        dk = dot_nn(ds, q) * FACTOR
        dq_ref[late * BLOCK:(late + 1) * BLOCK, cols] = (dot_nn(k.T, ds) * FACTOR).T.astype(jnp.bfloat16)
        if not late:
            early[h] = dk, dv
            before_ref[0, :, cols] = dk[:BEFORE].astype(jnp.bfloat16)
            before_ref[1, :, cols] = dv[:BEFORE].astype(jnp.bfloat16)
            return
        keep = SPAN - BEFORE
        for out_ref, first, second, i in ((dk_ref, early[h][0], dk, 0), (dv_ref, early[h][1], dv, 1)):
            out_ref[:keep, cols] = (first[BEFORE:] + second[:keep]).astype(jnp.bfloat16)
            out_ref[keep:, cols] = second[keep:TOK].astype(jnp.bfloat16)
            after_ref[i, :, cols] = second[TOK:TOK + SENT_AFTER].astype(jnp.bfloat16)

    units = [(h, late) for h in range(PER_STEP) for late in (0, 1)]
    ahead = products(*units[0])
    behind = None
    for i, unit in enumerate(units):
        now, ahead = ahead, products(*units[i + 1]) if i + 1 < len(units) else None
        done = differentiate(*unit, *now)
        if behind is not None:
            collect(*units[i - 1], *behind)
        behind = done
    collect(*units[-1], *behind)


def backward(half, start, end, lse_early, lse_late, q, g, k, v, before, after, *earlier):
    shape = jax.ShapeDtypeStruct
    steps = STEPS // 2
    first = half * steps
    lse = pl.BlockSpec((PER_STEP, 1, BLOCK), lambda i: (i + first, 0, 0))
    own = columns(TOK, first)
    return pl.pallas_call(
        backward_kernel,
        grid=(steps,),
        in_specs=[fixed((1, TOK)), fixed((1, TOK)), lse, lse, own, own,
                  own, columns(BEFORE, first), columns(AFTER, first),
                  own, columns(BEFORE, STEPS + first), columns(AFTER, STEPS + first)]
        + [pl.BlockSpec(memory_space=pl.ANY)] * len(earlier),
        out_specs=[own, own, own, halo_columns(BEFORE), halo_columns(SENT_AFTER)],
        out_shape=[shape((TOK, WIDTH), jnp.bfloat16)] * 3
        + [shape((2, BEFORE, WIDTH // 2), jnp.bfloat16), shape((2, SENT_AFTER, WIDTH // 2), jnp.bfloat16)],
        input_output_aliases={12 + i: i for i in range(len(earlier))},
        scratch_shapes=[pltpu.VMEM((2, SPAN, BLOCK), jnp.float32)],
        compiler_params=params(),
        cost_estimate=cost(10e9),
        name="attend_backward_second" if half else "attend_backward_first",
    )(start, end, lse_early, lse_late, q, g, k, before, after, v, before, after, *earlier)


def finish_kernel(dk_ref, dv_ref, prev_first_ref, prev_second_ref, next_first_ref, next_second_ref,
                  dk_out_ref, dv_out_ref):
    def add(prev_ref, next_ref):
        f32 = jnp.float32
        last = TOK - BEFORE
        for i, own_ref, out_ref in ((0, dk_ref, dk_out_ref), (1, dv_ref, dv_out_ref)):
            head = own_ref[:SENT_AFTER].astype(f32) + prev_ref[i].astype(f32)
            tail = own_ref[last:].astype(f32) + next_ref[i].astype(f32)
            out_ref[:SENT_AFTER] = head.astype(jnp.bfloat16)
            out_ref[SENT_AFTER:last] = own_ref[SENT_AFTER:last]
            out_ref[last:] = tail.astype(jnp.bfloat16)

    step = pl.program_id(0)
    pl.when(step < STEPS // 2)(lambda: add(prev_first_ref, next_first_ref))
    pl.when(step >= STEPS // 2)(lambda: add(prev_second_ref, next_second_ref))


def finish(dk, dv, from_prev, from_next):
    half = STEPS // 2

    def halo(rows, shift):
        return pl.BlockSpec((2, rows, COLS), lambda i: (0, 0, jnp.clip(i - shift, 0, half - 1)))

    return pl.pallas_call(
        finish_kernel,
        grid=(STEPS,),
        in_specs=[columns(TOK), columns(TOK), halo(SENT_AFTER, 0), halo(SENT_AFTER, half), halo(BEFORE, 0), halo(BEFORE, half)],
        out_specs=[columns(TOK)] * 2,
        out_shape=[jax.ShapeDtypeStruct((TOK, WIDTH), jnp.bfloat16)] * 2,
        compiler_params=params(),
        cost_estimate=cost(2e9),
        name="finish_grads",
    )(dk, dv, *from_prev, *from_next)


def scale_kernel(core_ref, mine_ref, other_ref, out_ref):
    core = core_ref[0]
    scale = float(TOKENS) ** -0.5
    out_ref[core] = mine_ref[...].astype(jnp.float32) * scale
    out_ref[1 - core] = other_ref[...].astype(jnp.float32) * scale


def scale_rows(core, mine, other):
    tile = 1024
    rows = pl.BlockSpec((HEAD_DIM, tile), lambda i, *_: (0, i))
    return pl.pallas_call(
        scale_kernel,
        grid_spec=pltpu.PrefetchScalarGridSpec(
            num_scalar_prefetch=1,
            grid=(WIDTH // tile,),
            in_specs=[rows, rows],
            out_specs=pl.BlockSpec((2, HEAD_DIM, tile), lambda i, *_: (0, 0, i)),
        ),
        out_shape=jax.ShapeDtypeStruct((2, HEAD_DIM, WIDTH), jnp.float32),
        compiler_params=params(),
        cost_estimate=cost(1e9),
        name="scale_rows",
    )(core, mine, other).reshape(2 * HEAD_DIM, WIDTH)


def weight_sums_kernel(core_ref, early_ref, late_ref, peer_early_ref, peer_late_ref, cot_ref, cot_peer_ref, out_ref):
    own = jnp.concatenate([early_ref[...], late_ref[...]], axis=0)
    peer = jnp.concatenate([peer_early_ref[...], peer_late_ref[...]], axis=0)
    core = core_ref[0]
    parts = [jnp.where(core == 0, own[:, 2 * j * HEAD_DIM:(2 * j + 1) * HEAD_DIM],
                       own[:, (2 * j + 1) * HEAD_DIM:(2 * j + 2) * HEAD_DIM]) for j in range(4)]
    own = jnp.concatenate(parts, axis=1)
    out_ref[...] = (dot_tn(own, cot_ref[...]) + dot_tn(peer, cot_peer_ref[...])).astype(jnp.bfloat16)


def weight_sums(core, early, late, peer_early, peer_late, cot, cot_peer):
    own_spec = pl.BlockSpec((BLOCK, 8 * HEAD_DIM), lambda i, *_: (0, i))
    peer_spec = pl.BlockSpec((BLOCK, 4 * HEAD_DIM), lambda i, *_: (0, i))
    return pl.pallas_call(
        weight_sums_kernel,
        grid_spec=pltpu.PrefetchScalarGridSpec(
            num_scalar_prefetch=1,
            grid=(2,),
            in_specs=[own_spec, own_spec, peer_spec, peer_spec, fixed((TOK, WIDTH)), fixed((TOK, WIDTH))],
            out_specs=pl.BlockSpec((4 * HEAD_DIM, WIDTH), lambda i, *_: (i, 0)),
        ),
        out_shape=jax.ShapeDtypeStruct((WIDTH // 2, WIDTH), jnp.bfloat16),
        compiler_params=params(),
        cost_estimate=cost(7e9),
        name="weight_sums",
    )(core, early, late, peer_early, peer_late, cot, cot_peer)


def place_weights(place_ref, refs, rows_ref):
    core = place_ref[0]
    zh = place_ref[1]
    near_ref, far_ref, near_other_ref, far_other_ref = refs
    rows_ref[:, zh, core] = near_ref[...]
    rows_ref[:, 1 - zh, core] = far_ref[...]
    rows_ref[:, zh, 1 - core] = near_other_ref[...]
    rows_ref[:, 1 - zh, 1 - core] = far_other_ref[...]


def grad_attn_kernel(place_ref, cot_ref, *refs):
    *weights, out_ref, rows_ref = refs
    place_weights(place_ref, weights, rows_ref)
    out_ref[...] = dot_nt(cot_ref[...], rows_ref[...].reshape(4 * HEAD_DIM, WIDTH)).astype(jnp.bfloat16)


def grad_attention(place, cot, *weights):
    piece = pl.BlockSpec((1, HEAD_DIM, WIDTH), lambda i, *_: (i, 0, 0))
    return pl.pallas_call(
        grad_attn_kernel,
        grid_spec=pltpu.PrefetchScalarGridSpec(
            num_scalar_prefetch=1,
            grid=(4,),
            in_specs=[fixed((TOK, WIDTH))] + [piece] * 4,
            out_specs=pl.BlockSpec((TOK, 4 * HEAD_DIM), lambda i, *_: (0, i)),
            scratch_shapes=[pltpu.VMEM((1, 2, 2, HEAD_DIM, WIDTH), jnp.bfloat16)],
        ),
        out_shape=jax.ShapeDtypeStruct((TOK, WIDTH), jnp.bfloat16),
        compiler_params=params(),
        cost_estimate=cost(7e9),
        name="grad_attention",
    )(place, cot, *weights)


def project_kernel(place_ref, early_ref, late_ref, *refs):
    *weights, out_ref, rows_ref, attn_ref = refs

    @pl.when(pl.program_id(0) == 0)
    def _():
        attn_ref[:BLOCK] = early_ref[...]
        attn_ref[BLOCK:] = late_ref[...]

    place_weights(place_ref, weights, rows_ref)
    out_ref[...] = dot_nn(attn_ref[...], rows_ref[...].reshape(WIDTH, out_ref.shape[1])).astype(jnp.bfloat16)


def project(place, early, late, *weights):
    tile = 512
    piece = pl.BlockSpec((4, HEAD_DIM, tile), lambda i, *_: (0, 0, i))
    return pl.pallas_call(
        project_kernel,
        grid_spec=pltpu.PrefetchScalarGridSpec(
            num_scalar_prefetch=1,
            grid=(WIDTH // tile,),
            in_specs=[fixed((BLOCK, WIDTH)), fixed((BLOCK, WIDTH))] + [piece] * 4,
            out_specs=pl.BlockSpec((TOK, tile), lambda i, *_: (0, i)),
            scratch_shapes=[pltpu.VMEM((4, 2, 2, HEAD_DIM, tile), jnp.bfloat16), pltpu.VMEM((TOK, WIDTH), jnp.bfloat16)],
        ),
        out_shape=jax.ShapeDtypeStruct((TOK, WIDTH), jnp.bfloat16),
        compiler_params=params(),
        cost_estimate=cost(8e9),
        name="project",
    )(place, early, late, *weights)


def sum_pieces_kernel(pieces_ref, out_ref):
    total = pieces_ref[0].astype(jnp.float32)
    for i in range(1, pieces_ref.shape[0]):
        total += pieces_ref[i].astype(jnp.float32)
    total = total.astype(jnp.bfloat16)
    for i in range(out_ref.shape[0]):
        out_ref[i] = total


def sum_pieces(pieces, copies, tile):
    count, rows, width = pieces.shape
    return pl.pallas_call(
        sum_pieces_kernel,
        grid=(rows // tile,),
        in_specs=[pl.BlockSpec((count, tile, width), lambda i: (0, i, 0))],
        out_specs=pl.BlockSpec((copies, tile, width), lambda i: (0, i, 0)),
        out_shape=jax.ShapeDtypeStruct((copies, rows, width), jnp.bfloat16),
        compiler_params=params(),
        cost_estimate=cost(2e9),
        name="sum_pieces",
    )(pieces)


def swapped(array):
    return lax.ppermute(array, "core", [(0, 1), (1, 0)])


def passed_along(array, by):
    devices = 16
    pairs = [(i, i + by) for i in range(devices) if 0 <= i + by < devices]
    return lax.ppermute(array, GROUP_AXES, pairs)


def across_z(array):
    return lax.ppermute(array, ("zh", "zl"), [(z, 3 - z) for z in range(4)])


def tied(array, *others):
    return lax.optimization_barrier((array, *others))[0]


def on_device(query_rows, key_rows, value_rows, pyramid_start, scale_end, out_weight, cotangent):
    core = lax.axis_index("core").astype(jnp.int32)
    group_index = lax.axis_index(GROUP_AXES).astype(jnp.int32)
    core_arg = core.reshape(1)
    place = jnp.stack([core, lax.axis_index("zh").astype(jnp.int32)])
    start = (pyramid_start - group_index * TOK).reshape(1, TOK)
    end = (scale_end - group_index * TOK).reshape(1, TOK)

    half = lax.dynamic_slice_in_dim(out_weight, core * HEAD_DIM, HEAD_DIM, 0)
    near_halves = jnp.broadcast_to(half, (4, HEAD_DIM, WIDTH))
    near = lax.all_to_all(near_halves, "y", 0, 0, tiled=True)
    far_half = across_z(half)
    after_rows = jnp.concatenate([key_rows[:AFTER], value_rows[:AFTER]], axis=1)
    after_rows = tied(after_rows, near_halves)
    after = passed_along(after_rows, -1)
    before_rows = jnp.concatenate([key_rows[TOK - BEFORE:], value_rows[TOK - BEFORE:]], axis=1)
    before = passed_along(tied(before_rows, after_rows, after), 1)
    cot_peer = swapped(tied(cotangent, after_rows))
    far_halves = jnp.broadcast_to(far_half, (4, HEAD_DIM, WIDTH))

    late, late_theirs, late_lse = forward(
        True, core_arg, start, end, tied(query_rows, far_halves), key_rows, value_rows, after)
    far = lax.all_to_all(tied(far_halves, near, late), "y", 0, 0, tiled=True)
    peer_late = swapped(late_theirs)
    early, early_theirs, early_lse = forward(
        False, core_arg, start, end, tied(query_rows, peer_late), key_rows, value_rows, before)
    peer_early = swapped(early_theirs)
    near_other = swapped(tied(near, late))
    sums = weight_sums(core_arg, early, late, peer_early, peer_late, cotangent, tied(cot_peer, near_other))
    far = tied(far, sums)
    pieces = lax.all_to_all(tied(sums.reshape(4, 2 * HEAD_DIM, WIDTH), far), "y", 0, 0, tiled=True)
    far_other = swapped(far)
    weights = (near, far, near_other, far_other)
    grad_attn = grad_attention(place, tied(cotangent, far), *weights)
    shared = (start, end, early_lse, late_lse, query_rows, grad_attn, key_rows, value_rows, before, after)
    dq, dk, dv, to_previous, to_next = backward(0, *shared)
    from_next = [passed_along(to_previous, -1)]
    from_prev = [passed_along(to_next, 1)]
    dq, dk, dv, to_previous, to_next = backward(1, *shared, dq, dk, dv)
    from_next.append(passed_along(to_previous, -1))
    from_prev.append(passed_along(to_next, 1))

    partial = tied(sum_pieces(tied(pieces, dk), 1, 128), from_prev[0], from_next[0]).reshape(16, 16, WIDTH)
    shares = lax.all_to_all(partial, ("zh", "x", "zl"), 0, 0, tiled=True)
    layer_out = project(place, tied(early, partial, from_next[1]), late, *weights)
    summed = sum_pieces(tied(shares, layer_out), 8, 16)
    rows_mine = lax.all_to_all(summed, ("x", "zl"), 0, 0, tiled=True).reshape(HEAD_DIM, WIDTH)
    key_grad, value_grad = finish(tied(dk, summed), dv, from_prev, from_next)
    rows_mine = tied(rows_mine, key_grad)
    weight_grad = scale_rows(core_arg, rows_mine, swapped(rows_mine))
    return (layer_out, dq, key_grad, value_grad, weight_grad)


def solution(mesh):
    inner = Mesh(mesh.devices.reshape(SIZES), AXES)
    rows = P(AXES, None)
    shard = P(("y", "zh"), None)
    return jax.shard_map(
        on_device,
        mesh=inner,
        in_specs=(rows, rows, rows, P(AXES), P(AXES), shard, rows),
        out_specs=(rows, rows, rows, rows, shard),
        check_vma=False,
    )
```

```python
import functools

import jax
import jax.numpy as jnp
from jax import lax
from jax.experimental import pallas as pl
from jax.experimental.pallas import tpu as pltpu
from jax.sharding import Mesh, PartitionSpec as P

HEADS = 16
HEAD_DIM = 128
WIDTH = HEADS * HEAD_DIM
TOK = 512
BLOCK = 256
BEFORE = 256
AFTER = 128
SENT_AFTER = 112
TOP = 96
SPAN = 640
FACTOR = HEAD_DIM ** -0.5
TOKENS = 65536

AXES = ("y", "zh", "x", "zl", "core")
SIZES = (4, 2, 4, 2, 2)
GROUP_AXES = ("x", "zl", "core")
MB = 1024 * 1024
PER_STEP = 4
STEPS = HEADS // PER_STEP
COLS = PER_STEP * HEAD_DIM


def dot_nt(left, right):
    return lax.dot_general(left, right, (((1,), (1,)), ((), ())), preferred_element_type=jnp.float32)


def dot_nn(left, right):
    return lax.dot_general(left, right, (((1,), (0,)), ((), ())), preferred_element_type=jnp.float32)


def dot_tn(left, right):
    return lax.dot_general(left, right, (((0,), (0,)), ((), ())), preferred_element_type=jnp.float32)


def fixed(shape):
    return pl.BlockSpec(shape, lambda i, *_: (0,) * len(shape))


def columns(rows, shift=0, row_block=0):
    return pl.BlockSpec((rows, COLS), lambda i, *_: (row_block, i + shift))


def halo_columns(rows):
    return pl.BlockSpec((2, rows, COLS), lambda i, *_: (0, 0, i))


def cost(flops):
    return pl.CostEstimate(flops=int(flops * 1e-3), bytes_accessed=0, transcendentals=0)


def params():
    return pltpu.CompilerParams(vmem_limit_bytes=56 * MB)


def fill_bias(late, start_ref, end_ref, bias_ref):
    first = 0 if late else -BEFORE
    pos = lax.broadcasted_iota(jnp.int32, (SPAN, BLOCK), 0) + first
    ok = (pos >= start_ref[...]) & (pos < end_ref[...])
    bias_ref[...] = jnp.where(ok, 0.0, -jnp.inf).astype(jnp.float32)


def gather_keys(late, own, halo):
    if late:
        return jnp.concatenate([own, halo], axis=0)
    return jnp.concatenate([halo, own[: SPAN - BEFORE]], axis=0)


HALVES = ((slice(0, 128), slice(0, 512)), (slice(128, 256), slice(128, 640)))


def assemble(first, second):
    none = jnp.zeros((SPAN - 512, 128), first.dtype)
    return jnp.concatenate([jnp.concatenate([first, none], axis=0), jnp.concatenate([none, second], axis=0)], axis=1)


def forward_kernel(core_ref, start_ref, end_ref, q_ref, ko_ref, kh_ref, vo_ref, vh_ref,
                   out_ref, theirs_ref, lse_ref, bias_ref, *, late):
    @pl.when(pl.program_id(0) == 0)
    def _():
        fill_bias(late, start_ref, end_ref, bias_ref)

    even = core_ref[0] == 0
    outs = []

    def head(h):
        return slice(h * HEAD_DIM, (h + 1) * HEAD_DIM)

    def scores(h):
        return dot_nt(gather_keys(late, ko_ref[:, head(h)], kh_ref[:, head(h)]), q_ref[:, head(h)])

    def weigh(s):
        parts = []
        for queries, keys in HALVES:
            part = s[keys, queries] + bias_ref[keys, queries]
            top = jnp.max(part, axis=0, keepdims=True)
            e = jnp.exp((part - top) * FACTOR)
            total = jnp.sum(e, axis=0, keepdims=True)
            parts.append((e.astype(jnp.bfloat16), top, total))
        first, second = parts
        return (assemble(first[0], second[0]), jnp.concatenate([first[1], second[1]], axis=1),
                jnp.concatenate([first[2], second[2]], axis=1))

    def mix(h, e, top, total):
        v = gather_keys(late, vo_ref[:, head(h)], vh_ref[:, head(h)])
        out = (dot_nn(v.T, e) * (1.0 / total)).T.astype(jnp.bfloat16)
        out_ref[:, head(h)] = out
        lse_ref[h] = top * FACTOR + jnp.log(total)
        outs.append(out)
        if h % 2:
            theirs_ref[:, head(h // 2)] = jnp.where(even, outs[h], outs[h - 1])

    ahead = scores(0)
    behind = None
    for h in range(PER_STEP):
        now, ahead = ahead, scores(h + 1) if h + 1 < PER_STEP else None
        weighed = weigh(now)
        if behind is not None:
            mix(h - 1, *behind)
        behind = weighed
    mix(PER_STEP - 1, *behind)


def forward(late, core, start, end, q, k, v, halo):
    row_block = 1 if late else 0
    halo_rows = AFTER if late else BEFORE
    bounds = pl.BlockSpec((1, BLOCK), lambda i, *_: (0, row_block))
    return pl.pallas_call(
        functools.partial(forward_kernel, late=late),
        grid_spec=pltpu.PrefetchScalarGridSpec(
            num_scalar_prefetch=1,
            grid=(STEPS,),
            in_specs=[bounds, bounds, columns(BLOCK, row_block=row_block),
                      columns(TOK), columns(halo_rows), columns(TOK), columns(halo_rows, STEPS)],
            out_specs=[columns(BLOCK),
                       pl.BlockSpec((BLOCK, COLS // 2), lambda i, *_: (0, i)),
                       pl.BlockSpec((PER_STEP, 1, BLOCK), lambda i, *_: (i, 0, 0))],
            scratch_shapes=[pltpu.VMEM((SPAN, BLOCK), jnp.float32)],
        ),
        out_shape=[jax.ShapeDtypeStruct((BLOCK, WIDTH), jnp.bfloat16),
                   jax.ShapeDtypeStruct((BLOCK, WIDTH // 2), jnp.bfloat16),
                   jax.ShapeDtypeStruct((HEADS, 1, BLOCK), jnp.float32)],
        compiler_params=params(),
        cost_estimate=cost(8e9),
        name="attend_late" if late else "attend_early",
    )(core, start, end, q, k, halo, v, halo)


def backward_kernel(start_ref, end_ref, lse_early_ref, lse_late_ref, q_ref, g_ref, ko_ref, kb_ref, ka_ref,
                    vo_ref, vb_ref, va_ref, *refs):
    dq_ref, dk_ref, dv_ref, before_ref, after_ref, bias_ref = refs[-6:]

    @pl.when(pl.program_id(0) == 0)
    def _():
        for late in (False, True):
            block = slice(BLOCK, 2 * BLOCK) if late else slice(0, BLOCK)
            fill_bias(late, start_ref.at[:, block], end_ref.at[:, block], bias_ref.at[int(late)])

    def head(h):
        return slice(h * HEAD_DIM, (h + 1) * HEAD_DIM)

    def products(h, late):
        cols = head(h)
        halves = (ka_ref, va_ref) if late else (kb_ref, vb_ref)
        k = gather_keys(late, ko_ref[:, cols], halves[0][:, cols])
        v = gather_keys(late, vo_ref[:, cols], halves[1][:, cols])
        q = q_ref[late * BLOCK:(late + 1) * BLOCK, cols]
        g = g_ref[late * BLOCK:(late + 1) * BLOCK, cols]
        return k, q, g, [(dot_nt(k[keys], q[queries]), dot_nt(v[keys], g[queries])) for queries, keys in HALVES]

    def differentiate(h, late, k, q, g, pairs):
        lse_ref = lse_late_ref if late else lse_early_ref
        probs = []
        grads = []
        for (queries, keys), (s, dp) in zip(HALVES, pairs):
            p = jnp.exp((s + bias_ref[late, keys, queries]) * FACTOR - lse_ref[h, :, queries])
            inner = jnp.sum(p * dp, axis=0, keepdims=True)
            probs.append(p.astype(jnp.bfloat16))
            grads.append((p * (dp - inner)).astype(jnp.bfloat16))
        return k, q, g, assemble(*probs), assemble(*grads)

    early = {}

    def collect(h, late, k, q, g, p, ds):
        cols = head(h)
        dv = dot_nn(p, g)
        dk = dot_nn(ds, q) * FACTOR
        dq_ref[late * BLOCK:(late + 1) * BLOCK, cols] = (dot_nn(k.T, ds) * FACTOR).T.astype(jnp.bfloat16)
        if not late:
            early[h] = dk, dv
            before_ref[0, :, cols] = dk[:BEFORE].astype(jnp.bfloat16)
            before_ref[1, :, cols] = dv[:BEFORE].astype(jnp.bfloat16)
            return
        keep = SPAN - BEFORE
        for out_ref, first, second, i in ((dk_ref, early[h][0], dk, 0), (dv_ref, early[h][1], dv, 1)):
            out_ref[:keep, cols] = (first[BEFORE:] + second[:keep]).astype(jnp.bfloat16)
            out_ref[keep:, cols] = second[keep:TOK].astype(jnp.bfloat16)
            after_ref[i, :, cols] = second[TOK:TOK + SENT_AFTER].astype(jnp.bfloat16)

    units = [(h, late) for h in range(PER_STEP) for late in (0, 1)]
    ahead = products(*units[0])
    behind = None
    for i, unit in enumerate(units):
        now, ahead = ahead, products(*units[i + 1]) if i + 1 < len(units) else None
        done = differentiate(*unit, *now)
        if behind is not None:
            collect(*units[i - 1], *behind)
        behind = done
    collect(*units[-1], *behind)


def backward(half, start, end, lse_early, lse_late, q, g, k, v, before, after, *earlier):
    shape = jax.ShapeDtypeStruct
    steps = STEPS // 2
    first = half * steps
    lse = pl.BlockSpec((PER_STEP, 1, BLOCK), lambda i: (i + first, 0, 0))
    own = columns(TOK, first)
    return pl.pallas_call(
        backward_kernel,
        grid=(steps,),
        in_specs=[fixed((1, TOK)), fixed((1, TOK)), lse, lse, own, own,
                  own, columns(BEFORE, first), columns(AFTER, first),
                  own, columns(BEFORE, STEPS + first), columns(AFTER, STEPS + first)]
        + [pl.BlockSpec(memory_space=pl.ANY)] * len(earlier),
        out_specs=[own, own, own, halo_columns(BEFORE), halo_columns(SENT_AFTER)],
        out_shape=[shape((TOK, WIDTH), jnp.bfloat16)] * 3
        + [shape((2, BEFORE, WIDTH // 2), jnp.bfloat16), shape((2, SENT_AFTER, WIDTH // 2), jnp.bfloat16)],
        input_output_aliases={12 + i: i for i in range(len(earlier))},
        scratch_shapes=[pltpu.VMEM((2, SPAN, BLOCK), jnp.float32)],
        compiler_params=params(),
        cost_estimate=cost(10e9),
        name="attend_backward_second" if half else "attend_backward_first",
    )(start, end, lse_early, lse_late, q, g, k, before, after, v, before, after, *earlier)


def finish_kernel(dk_ref, dv_ref, first_ref, second_ref, dk_out_ref, dv_out_ref):
    def add(halo_ref):
        for i, own_ref, out_ref in ((0, dk_ref, dk_out_ref), (1, dv_ref, dv_out_ref)):
            total = own_ref[...].astype(jnp.float32) + halo_ref[i].astype(jnp.float32)
            out_ref[...] = total.astype(jnp.bfloat16)

    step = pl.program_id(0)
    pl.when(step < STEPS // 2)(lambda: add(first_ref))
    pl.when(step >= STEPS // 2)(lambda: add(second_ref))


def finish(dk, dv, first, second):
    rows = first.shape[1]
    half = STEPS // 2
    part = columns(rows, row_block=(TOK - rows) // rows if rows == BEFORE else 0)
    return pl.pallas_call(
        finish_kernel,
        grid=(STEPS,),
        in_specs=[part, part,
                  pl.BlockSpec((2, rows, COLS), lambda i: (0, 0, jnp.minimum(i, half - 1))),
                  pl.BlockSpec((2, rows, COLS), lambda i: (0, 0, jnp.maximum(i - half, 0)))],
        out_specs=[part, part],
        out_shape=[jax.ShapeDtypeStruct((TOK, WIDTH), jnp.bfloat16)] * 2,
        input_output_aliases={0: 0, 1: 1},
        compiler_params=params(),
        cost_estimate=cost(2e9),
        name="finish_grads",
    )(dk, dv, first, second)


def weight_sums_kernel(core_ref, early_ref, late_ref, peer_early_ref, peer_late_ref, cot_ref, cot_peer_ref, out_ref):
    own = jnp.concatenate([early_ref[...], late_ref[...]], axis=0)
    peer = jnp.concatenate([peer_early_ref[...], peer_late_ref[...]], axis=0)
    core = core_ref[0]
    parts = [jnp.where(core == 0, own[:, 2 * j * HEAD_DIM:(2 * j + 1) * HEAD_DIM],
                       own[:, (2 * j + 1) * HEAD_DIM:(2 * j + 2) * HEAD_DIM]) for j in range(4)]
    own = jnp.concatenate(parts, axis=1)
    out_ref[...] = (dot_tn(own, cot_ref[...]) + dot_tn(peer, cot_peer_ref[...])).astype(jnp.bfloat16)


def weight_sums(core, early, late, peer_early, peer_late, cot, cot_peer):
    own_spec = pl.BlockSpec((BLOCK, 8 * HEAD_DIM), lambda i, *_: (0, i))
    peer_spec = pl.BlockSpec((BLOCK, 4 * HEAD_DIM), lambda i, *_: (0, i))
    return pl.pallas_call(
        weight_sums_kernel,
        grid_spec=pltpu.PrefetchScalarGridSpec(
            num_scalar_prefetch=1,
            grid=(2,),
            in_specs=[own_spec, own_spec, peer_spec, peer_spec, fixed((TOK, WIDTH)), fixed((TOK, WIDTH))],
            out_specs=pl.BlockSpec((4 * HEAD_DIM, WIDTH), lambda i, *_: (i, 0)),
        ),
        out_shape=jax.ShapeDtypeStruct((WIDTH // 2, WIDTH), jnp.bfloat16),
        compiler_params=params(),
        cost_estimate=cost(7e9),
        name="weight_sums",
    )(core, early, late, peer_early, peer_late, cot, cot_peer)


def place_weights(place_ref, refs, rows_ref):
    core = place_ref[0]
    zh = place_ref[1]
    for at, (near_ref, top_ref, low_ref) in ((core, refs[:3]), (1 - core, refs[3:])):
        rows_ref[:, zh, at] = near_ref[...]
        rows_ref[:, 1 - zh, at, :TOP] = top_ref[...]
        rows_ref[:, 1 - zh, at, TOP:] = low_ref[...]


def grad_attn_kernel(place_ref, cot_ref, *refs):
    *weights, out_ref, rows_ref = refs
    place_weights(place_ref, weights, rows_ref)
    out_ref[...] = dot_nt(cot_ref[...], rows_ref[...].reshape(4 * HEAD_DIM, WIDTH)).astype(jnp.bfloat16)


def grad_attention(place, cot, *weights):
    pieces = [pl.BlockSpec((1, rows, WIDTH), lambda i, *_: (i, 0, 0)) for rows in (HEAD_DIM, TOP, HEAD_DIM - TOP)]
    return pl.pallas_call(
        grad_attn_kernel,
        grid_spec=pltpu.PrefetchScalarGridSpec(
            num_scalar_prefetch=1,
            grid=(4,),
            in_specs=[fixed((TOK, WIDTH))] + pieces * 2,
            out_specs=pl.BlockSpec((TOK, 4 * HEAD_DIM), lambda i, *_: (0, i)),
            scratch_shapes=[pltpu.VMEM((1, 2, 2, HEAD_DIM, WIDTH), jnp.bfloat16)],
        ),
        out_shape=jax.ShapeDtypeStruct((TOK, WIDTH), jnp.bfloat16),
        compiler_params=params(),
        cost_estimate=cost(7e9),
        name="grad_attention",
    )(place, cot, *weights)


def project_kernel(place_ref, early_ref, late_ref, *refs):
    *weights, out_ref, rows_ref, attn_ref = refs

    @pl.when(pl.program_id(0) == 0)
    def _():
        attn_ref[:BLOCK] = early_ref[...]
        attn_ref[BLOCK:] = late_ref[...]

    place_weights(place_ref, weights, rows_ref)
    out_ref[...] = dot_nn(attn_ref[...], rows_ref[...].reshape(WIDTH, out_ref.shape[1])).astype(jnp.bfloat16)


def project(place, early, late, *weights):
    tile = 512
    pieces = [pl.BlockSpec((4, rows, tile), lambda i, *_: (0, 0, i)) for rows in (HEAD_DIM, TOP, HEAD_DIM - TOP)]
    return pl.pallas_call(
        project_kernel,
        grid_spec=pltpu.PrefetchScalarGridSpec(
            num_scalar_prefetch=1,
            grid=(WIDTH // tile,),
            in_specs=[fixed((BLOCK, WIDTH)), fixed((BLOCK, WIDTH))] + pieces * 2,
            out_specs=pl.BlockSpec((TOK, tile), lambda i, *_: (0, i)),
            scratch_shapes=[pltpu.VMEM((4, 2, 2, HEAD_DIM, tile), jnp.bfloat16), pltpu.VMEM((TOK, WIDTH), jnp.bfloat16)],
        ),
        out_shape=jax.ShapeDtypeStruct((TOK, WIDTH), jnp.bfloat16),
        compiler_params=params(),
        cost_estimate=cost(8e9),
        name="project",
    )(place, early, late, *weights)


def sum_pieces_kernel(pieces_ref, out_ref):
    total = pieces_ref[0].astype(jnp.float32)
    for i in range(1, pieces_ref.shape[0]):
        total += pieces_ref[i].astype(jnp.float32)
    total = total.astype(jnp.bfloat16)
    for i in range(out_ref.shape[0]):
        out_ref[i] = total


def sum_pieces(pieces, copies, tile):
    count, rows, width = pieces.shape
    return pl.pallas_call(
        sum_pieces_kernel,
        grid=(rows // tile,),
        in_specs=[pl.BlockSpec((count, tile, width), lambda i: (0, i, 0))],
        out_specs=pl.BlockSpec((copies, tile, width), lambda i: (0, i, 0)),
        out_shape=jax.ShapeDtypeStruct((copies, rows, width), jnp.bfloat16),
        compiler_params=params(),
        cost_estimate=cost(2e9),
        name="sum_pieces",
    )(pieces)


def copy_kernel(in_ref, out_ref):
    out_ref[...] = in_ref[...]


def low_rows(near):
    y, rows, width = near.shape
    low = rows - TOP
    return pl.pallas_call(
        copy_kernel,
        grid=(2,),
        in_specs=[pl.BlockSpec((y // 2, low, width), lambda i: (i, TOP // low, 0))],
        out_specs=pl.BlockSpec((y // 2, low, width), lambda i: (i, 0, 0)),
        out_shape=jax.ShapeDtypeStruct((y, low, width), near.dtype),
        compiler_params=params(),
        cost_estimate=cost(1e9),
        name="low_rows",
    )(near)


def swapped(array):
    return lax.ppermute(array, "core", [(0, 1), (1, 0)])


def passed_along(array, by):
    devices = 16
    pairs = [(i, i + by) for i in range(devices) if 0 <= i + by < devices]
    return lax.ppermute(array, GROUP_AXES, pairs)


def across_z(array):
    return lax.ppermute(array, ("zh", "zl"), [(z, 3 - z) for z in range(4)])


def tied(array, *others):
    return lax.optimization_barrier((array, *others))[0]


def on_device(query_rows, key_rows, value_rows, pyramid_start, scale_end, out_weight, cotangent):
    core = lax.axis_index("core").astype(jnp.int32)
    group_index = lax.axis_index(GROUP_AXES).astype(jnp.int32)
    core_arg = core.reshape(1)
    place = jnp.stack([core, lax.axis_index("zh").astype(jnp.int32)])
    start = (pyramid_start - group_index * TOK).reshape(1, TOK)
    end = (scale_end - group_index * TOK).reshape(1, TOK)

    half = lax.dynamic_slice_in_dim(out_weight, core * HEAD_DIM, HEAD_DIM, 0)
    near_halves = jnp.broadcast_to(half, (4, HEAD_DIM, WIDTH))
    near = lax.all_to_all(near_halves, "y", 0, 0, tiled=True)
    far_half = across_z(half)
    after_rows = jnp.concatenate([key_rows[:AFTER], value_rows[:AFTER]], axis=1)
    after_rows = tied(after_rows, near_halves)
    after = passed_along(after_rows, -1)
    before_rows = jnp.concatenate([key_rows[TOK - BEFORE:], value_rows[TOK - BEFORE:]], axis=1)
    before = passed_along(tied(before_rows, after_rows, after), 1)
    cot_peer = swapped(tied(cotangent, after_rows))
    far_tops = jnp.broadcast_to(far_half[:TOP], (4, TOP, WIDTH))

    late, late_theirs, late_lse = forward(
        True, core_arg, start, end, tied(query_rows, far_tops), key_rows, value_rows, after)
    far_top = lax.all_to_all(tied(far_tops, near, late), "y", 0, 0, tiled=True)
    low = low_rows(tied(near, late))
    far_low = across_z(low)
    peer_late = swapped(late_theirs)
    early, early_theirs, early_lse = forward(
        False, core_arg, start, end, tied(query_rows, peer_late, low), key_rows, value_rows, before)
    peer_early = swapped(early_theirs)
    near_other = swapped(tied(near, late))
    sums = weight_sums(core_arg, early, late, peer_early, peer_late, cotangent, tied(cot_peer, near_other))
    far_top = tied(far_top, sums)
    far_low = tied(far_low, sums)
    pieces = lax.all_to_all(tied(sums.reshape(4, 2 * HEAD_DIM, WIDTH), far_top), "y", 0, 0, tiled=True)
    weights = (near, far_top, far_low, near_other, swapped(far_top), swapped(far_low))
    grad_attn = grad_attention(place, tied(cotangent, far_top), *weights)
    shared = (start, end, early_lse, late_lse, query_rows, grad_attn, key_rows, value_rows, before, after)
    dq, dk, dv, to_previous, to_next = backward(0, *shared)
    from_next = [passed_along(to_previous, -1)]
    from_prev = [passed_along(to_next, 1)]
    dq, dk, dv, to_previous, to_next = backward(1, *shared, dq, dk, dv)
    from_next.append(passed_along(to_previous, -1))
    from_prev.append(passed_along(to_next, 1))

    partial = tied(sum_pieces(tied(pieces, dk), 1, 128), from_prev[0], from_next[0]).reshape(16, 16, WIDTH)
    shares = lax.all_to_all(partial, ("zh", "x", "zl"), 0, 0, tiled=True)
    layer_out = project(place, tied(early, partial, from_next[1]), late, *weights)
    summed = sum_pieces(tied(shares, layer_out), 8, 16)
    rows_mine = lax.all_to_all(summed, ("x", "zl"), 0, 0, tiled=True).reshape(HEAD_DIM, WIDTH)
    dk, dv = finish(tied(dk, summed), dv, *from_prev)
    key_grad, value_grad = finish(dk, dv, *from_next)
    rows_mine = tied(rows_mine, key_grad)
    rows_other = swapped(rows_mine)
    first = jnp.where(core == 0, rows_mine, rows_other)
    second = jnp.where(core == 0, rows_other, rows_mine)
    weight_grad = jnp.concatenate([first, second], axis=0).astype(jnp.float32) * (float(TOKENS) ** -0.5)
    return (layer_out, dq, key_grad, value_grad, weight_grad)


def solution(mesh):
    inner = Mesh(mesh.devices.reshape(SIZES), AXES)
    rows = P(AXES, None)
    shard = P(("y", "zh"), None)
    return jax.shard_map(
        on_device,
        mesh=inner,
        in_specs=(rows, rows, rows, P(AXES), P(AXES), shard, rows),
        out_specs=(rows, rows, rows, rows, shard),
        check_vma=False,
    )
```

```python
import functools

import jax
import jax.numpy as jnp
from jax import lax
from jax.experimental import pallas as pl
from jax.experimental.pallas import tpu as pltpu
from jax.sharding import Mesh, PartitionSpec as P

HEADS = 16
HEAD_DIM = 128
WIDTH = HEADS * HEAD_DIM
TOK = 512
BLOCK = 256
BEFORE = 256
AFTER = 128
SENT_AFTER = 112
SPAN = 640
FACTOR = HEAD_DIM ** -0.5
TOKENS = 65536

AXES = ("y", "zh", "x", "zl", "core")
SIZES = (4, 2, 4, 2, 2)
GROUP_AXES = ("x", "zl", "core")
MB = 1024 * 1024
PER_STEP = 4
STEPS = HEADS // PER_STEP
COLS = PER_STEP * HEAD_DIM


def dot_nt(left, right):
    return lax.dot_general(left, right, (((1,), (1,)), ((), ())), preferred_element_type=jnp.float32)


def dot_nn(left, right):
    return lax.dot_general(left, right, (((1,), (0,)), ((), ())), preferred_element_type=jnp.float32)


def dot_tn(left, right):
    return lax.dot_general(left, right, (((0,), (0,)), ((), ())), preferred_element_type=jnp.float32)


def fixed(shape):
    return pl.BlockSpec(shape, lambda i, *_: (0,) * len(shape))


def columns(rows, shift=0, row_block=0):
    return pl.BlockSpec((rows, COLS), lambda i, *_: (row_block, i + shift))


def halo_columns(rows):
    return pl.BlockSpec((2, rows, COLS), lambda i, *_: (0, 0, i))


def cost(flops):
    return pl.CostEstimate(flops=int(flops * 1e-3), bytes_accessed=0, transcendentals=0)


def params():
    return pltpu.CompilerParams(vmem_limit_bytes=56 * MB)


def fill_bias(late, start_ref, end_ref, bias_ref):
    first = 0 if late else -BEFORE
    pos = lax.broadcasted_iota(jnp.int32, (SPAN, BLOCK), 0) + first
    ok = (pos >= start_ref[...]) & (pos < end_ref[...])
    bias_ref[...] = jnp.where(ok, 0.0, -jnp.inf).astype(jnp.float32)


def gather_keys(late, own, halo):
    if late:
        return jnp.concatenate([own, halo], axis=0)
    return jnp.concatenate([halo, own[: SPAN - BEFORE]], axis=0)


HALVES = ((slice(0, 128), slice(0, 512)), (slice(128, 256), slice(128, 640)))


def assemble(first, second):
    none = jnp.zeros((SPAN - 512, 128), first.dtype)
    return jnp.concatenate([jnp.concatenate([first, none], axis=0), jnp.concatenate([none, second], axis=0)], axis=1)


def forward_kernel(core_ref, start_ref, end_ref, q_ref, ko_ref, kh_ref, vo_ref, vh_ref,
                   out_ref, theirs_ref, lse_ref, bias_ref, *, late):
    @pl.when(pl.program_id(0) == 0)
    def _():
        fill_bias(late, start_ref, end_ref, bias_ref)

    even = core_ref[0] == 0
    outs = []

    def head(h):
        return slice(h * HEAD_DIM, (h + 1) * HEAD_DIM)

    def scores(h):
        return dot_nt(gather_keys(late, ko_ref[:, head(h)], kh_ref[:, head(h)]), q_ref[:, head(h)])

    def weigh(s):
        parts = []
        for queries, keys in HALVES:
            part = s[keys, queries] + bias_ref[keys, queries]
            top = jnp.max(part, axis=0, keepdims=True)
            e = jnp.exp((part - top) * FACTOR)
            total = jnp.sum(e, axis=0, keepdims=True)
            parts.append((e.astype(jnp.bfloat16), top, total))
        first, second = parts
        return (assemble(first[0], second[0]), jnp.concatenate([first[1], second[1]], axis=1),
                jnp.concatenate([first[2], second[2]], axis=1))

    def mix(h, e, top, total):
        v = gather_keys(late, vo_ref[:, head(h)], vh_ref[:, head(h)])
        out = (dot_nn(v.T, e) * (1.0 / total)).T.astype(jnp.bfloat16)
        out_ref[:, head(h)] = out
        lse_ref[h] = top * FACTOR + jnp.log(total)
        outs.append(out)
        if h % 2:
            theirs_ref[:, head(h // 2)] = jnp.where(even, outs[h], outs[h - 1])

    ahead = scores(0)
    behind = None
    for h in range(PER_STEP):
        now, ahead = ahead, scores(h + 1) if h + 1 < PER_STEP else None
        weighed = weigh(now)
        if behind is not None:
            mix(h - 1, *behind)
        behind = weighed
    mix(PER_STEP - 1, *behind)


def forward(late, core, start, end, q, k, v, halo):
    row_block = 1 if late else 0
    halo_rows = AFTER if late else BEFORE
    bounds = pl.BlockSpec((1, BLOCK), lambda i, *_: (0, row_block))
    return pl.pallas_call(
        functools.partial(forward_kernel, late=late),
        grid_spec=pltpu.PrefetchScalarGridSpec(
            num_scalar_prefetch=1,
            grid=(STEPS,),
            in_specs=[bounds, bounds, columns(BLOCK, row_block=row_block),
                      columns(TOK), columns(halo_rows), columns(TOK), columns(halo_rows, STEPS)],
            out_specs=[columns(BLOCK),
                       pl.BlockSpec((BLOCK, COLS // 2), lambda i, *_: (0, i)),
                       pl.BlockSpec((PER_STEP, 1, BLOCK), lambda i, *_: (i, 0, 0))],
            scratch_shapes=[pltpu.VMEM((SPAN, BLOCK), jnp.float32)],
        ),
        out_shape=[jax.ShapeDtypeStruct((BLOCK, WIDTH), jnp.bfloat16),
                   jax.ShapeDtypeStruct((BLOCK, WIDTH // 2), jnp.bfloat16),
                   jax.ShapeDtypeStruct((HEADS, 1, BLOCK), jnp.float32)],
        compiler_params=params(),
        cost_estimate=cost(8e9),
        name="attend_late" if late else "attend_early",
    )(core, start, end, q, k, halo, v, halo)


def backward_kernel(start_ref, end_ref, lse_early_ref, lse_late_ref, q_ref, g_ref, ko_ref, kb_ref, ka_ref,
                    vo_ref, vb_ref, va_ref, *refs):
    dq_ref, dk_ref, dv_ref, before_ref, after_ref, bias_ref = refs[-6:]

    @pl.when(pl.program_id(0) == 0)
    def _():
        for late in (False, True):
            block = slice(BLOCK, 2 * BLOCK) if late else slice(0, BLOCK)
            fill_bias(late, start_ref.at[:, block], end_ref.at[:, block], bias_ref.at[int(late)])

    def head(h):
        return slice(h * HEAD_DIM, (h + 1) * HEAD_DIM)

    def products(h, late):
        cols = head(h)
        halves = (ka_ref, va_ref) if late else (kb_ref, vb_ref)
        k = gather_keys(late, ko_ref[:, cols], halves[0][:, cols])
        v = gather_keys(late, vo_ref[:, cols], halves[1][:, cols])
        q = q_ref[late * BLOCK:(late + 1) * BLOCK, cols]
        g = g_ref[late * BLOCK:(late + 1) * BLOCK, cols]
        return k, q, g, [(dot_nt(k[keys], q[queries]), dot_nt(v[keys], g[queries])) for queries, keys in HALVES]

    def differentiate(h, late, k, q, g, pairs):
        lse_ref = lse_late_ref if late else lse_early_ref
        probs = []
        grads = []
        for (queries, keys), (s, dp) in zip(HALVES, pairs):
            p = jnp.exp((s + bias_ref[late, keys, queries]) * FACTOR - lse_ref[h, :, queries])
            inner = jnp.sum(p * dp, axis=0, keepdims=True)
            probs.append(p.astype(jnp.bfloat16))
            grads.append((p * (dp - inner)).astype(jnp.bfloat16))
        return k, q, g, assemble(*probs), assemble(*grads)

    early = {}

    def collect(h, late, k, q, g, p, ds):
        cols = head(h)
        dv = dot_nn(p, g)
        dk = dot_nn(ds, q) * FACTOR
        dq_ref[late * BLOCK:(late + 1) * BLOCK, cols] = (dot_nn(k.T, ds) * FACTOR).T.astype(jnp.bfloat16)
        if not late:
            early[h] = dk, dv
            before_ref[0, :, cols] = dk[:BEFORE].astype(jnp.bfloat16)
            before_ref[1, :, cols] = dv[:BEFORE].astype(jnp.bfloat16)
            return
        keep = SPAN - BEFORE
        for out_ref, first, second, i in ((dk_ref, early[h][0], dk, 0), (dv_ref, early[h][1], dv, 1)):
            out_ref[:keep, cols] = (first[BEFORE:] + second[:keep]).astype(jnp.bfloat16)
            out_ref[keep:, cols] = second[keep:TOK].astype(jnp.bfloat16)
            after_ref[i, :, cols] = second[TOK:TOK + SENT_AFTER].astype(jnp.bfloat16)

    units = [(h, late) for h in range(PER_STEP) for late in (0, 1)]
    ahead = products(*units[0])
    behind = None
    for i, unit in enumerate(units):
        now, ahead = ahead, products(*units[i + 1]) if i + 1 < len(units) else None
        done = differentiate(*unit, *now)
        if behind is not None:
            collect(*units[i - 1], *behind)
        behind = done
    collect(*units[-1], *behind)


def backward(half, start, end, lse_early, lse_late, q, g, k, v, before, after, *earlier):
    shape = jax.ShapeDtypeStruct
    steps = STEPS // 2
    first = half * steps
    lse = pl.BlockSpec((PER_STEP, 1, BLOCK), lambda i: (i + first, 0, 0))
    own = columns(TOK, first)
    return pl.pallas_call(
        backward_kernel,
        grid=(steps,),
        in_specs=[fixed((1, TOK)), fixed((1, TOK)), lse, lse, own, own,
                  own, columns(BEFORE, first), columns(AFTER, first),
                  own, columns(BEFORE, STEPS + first), columns(AFTER, STEPS + first)]
        + [pl.BlockSpec(memory_space=pl.ANY)] * len(earlier),
        out_specs=[own, own, own, halo_columns(BEFORE), halo_columns(SENT_AFTER)],
        out_shape=[shape((TOK, WIDTH), jnp.bfloat16)] * 3
        + [shape((2, BEFORE, WIDTH // 2), jnp.bfloat16), shape((2, SENT_AFTER, WIDTH // 2), jnp.bfloat16)],
        input_output_aliases={12 + i: i for i in range(len(earlier))},
        scratch_shapes=[pltpu.VMEM((2, SPAN, BLOCK), jnp.float32)],
        compiler_params=params(),
        cost_estimate=cost(10e9),
        name="attend_backward_second" if half else "attend_backward_first",
    )(start, end, lse_early, lse_late, q, g, k, before, after, v, before, after, *earlier)


def finish_kernel(dk_ref, dv_ref, prev_first_ref, prev_second_ref, next_first_ref, next_second_ref,
                  dk_out_ref, dv_out_ref):
    def add(prev_ref, next_ref):
        f32 = jnp.float32
        last = TOK - BEFORE
        for i, own_ref, out_ref in ((0, dk_ref, dk_out_ref), (1, dv_ref, dv_out_ref)):
            head = own_ref[:SENT_AFTER].astype(f32) + prev_ref[i].astype(f32)
            tail = own_ref[last:].astype(f32) + next_ref[i].astype(f32)
            out_ref[:SENT_AFTER] = head.astype(jnp.bfloat16)
            out_ref[SENT_AFTER:last] = own_ref[SENT_AFTER:last]
            out_ref[last:] = tail.astype(jnp.bfloat16)

    step = pl.program_id(0)
    pl.when(step < STEPS // 2)(lambda: add(prev_first_ref, next_first_ref))
    pl.when(step >= STEPS // 2)(lambda: add(prev_second_ref, next_second_ref))


def finish(dk, dv, from_prev, from_next):
    half = STEPS // 2

    def halo(rows, shift):
        return pl.BlockSpec((2, rows, COLS), lambda i: (0, 0, jnp.clip(i - shift, 0, half - 1)))

    return pl.pallas_call(
        finish_kernel,
        grid=(STEPS,),
        in_specs=[columns(TOK), columns(TOK), halo(SENT_AFTER, 0), halo(SENT_AFTER, half), halo(BEFORE, 0), halo(BEFORE, half)],
        out_specs=[columns(TOK)] * 2,
        out_shape=[jax.ShapeDtypeStruct((TOK, WIDTH), jnp.bfloat16)] * 2,
        compiler_params=params(),
        cost_estimate=cost(2e9),
        name="finish_grads",
    )(dk, dv, *from_prev, *from_next)


def weight_sums_kernel(core_ref, early_ref, late_ref, peer_early_ref, peer_late_ref, cot_ref, cot_peer_ref, out_ref):
    own = jnp.concatenate([early_ref[...], late_ref[...]], axis=0)
    peer = jnp.concatenate([peer_early_ref[...], peer_late_ref[...]], axis=0)
    core = core_ref[0]
    parts = [jnp.where(core == 0, own[:, 2 * j * HEAD_DIM:(2 * j + 1) * HEAD_DIM],
                       own[:, (2 * j + 1) * HEAD_DIM:(2 * j + 2) * HEAD_DIM]) for j in range(4)]
    own = jnp.concatenate(parts, axis=1)
    out_ref[...] = (dot_tn(own, cot_ref[...]) + dot_tn(peer, cot_peer_ref[...])).astype(jnp.bfloat16)


def weight_sums(core, early, late, peer_early, peer_late, cot, cot_peer):
    own_spec = pl.BlockSpec((BLOCK, 8 * HEAD_DIM), lambda i, *_: (0, i))
    peer_spec = pl.BlockSpec((BLOCK, 4 * HEAD_DIM), lambda i, *_: (0, i))
    return pl.pallas_call(
        weight_sums_kernel,
        grid_spec=pltpu.PrefetchScalarGridSpec(
            num_scalar_prefetch=1,
            grid=(2,),
            in_specs=[own_spec, own_spec, peer_spec, peer_spec, fixed((TOK, WIDTH)), fixed((TOK, WIDTH))],
            out_specs=pl.BlockSpec((4 * HEAD_DIM, WIDTH), lambda i, *_: (i, 0)),
        ),
        out_shape=jax.ShapeDtypeStruct((WIDTH // 2, WIDTH), jnp.bfloat16),
        compiler_params=params(),
        cost_estimate=cost(7e9),
        name="weight_sums",
    )(core, early, late, peer_early, peer_late, cot, cot_peer)


def place_weights(place_ref, refs, rows_ref):
    core = place_ref[0]
    zh = place_ref[1]
    near_ref, far_ref, near_other_ref, far_other_ref = refs
    rows_ref[:, zh, core] = near_ref[...]
    rows_ref[:, 1 - zh, core] = far_ref[...]
    rows_ref[:, zh, 1 - core] = near_other_ref[...]
    rows_ref[:, 1 - zh, 1 - core] = far_other_ref[...]


def grad_attn_kernel(place_ref, cot_ref, *refs):
    *weights, out_ref, rows_ref = refs
    place_weights(place_ref, weights, rows_ref)
    out_ref[...] = dot_nt(cot_ref[...], rows_ref[...].reshape(4 * HEAD_DIM, WIDTH)).astype(jnp.bfloat16)


def grad_attention(place, cot, *weights):
    piece = pl.BlockSpec((1, HEAD_DIM, WIDTH), lambda i, *_: (i, 0, 0))
    return pl.pallas_call(
        grad_attn_kernel,
        grid_spec=pltpu.PrefetchScalarGridSpec(
            num_scalar_prefetch=1,
            grid=(4,),
            in_specs=[fixed((TOK, WIDTH))] + [piece] * 4,
            out_specs=pl.BlockSpec((TOK, 4 * HEAD_DIM), lambda i, *_: (0, i)),
            scratch_shapes=[pltpu.VMEM((1, 2, 2, HEAD_DIM, WIDTH), jnp.bfloat16)],
        ),
        out_shape=jax.ShapeDtypeStruct((TOK, WIDTH), jnp.bfloat16),
        compiler_params=params(),
        cost_estimate=cost(7e9),
        name="grad_attention",
    )(place, cot, *weights)


def project_kernel(place_ref, early_ref, late_ref, *refs):
    *weights, out_ref, rows_ref, attn_ref = refs

    @pl.when(pl.program_id(0) == 0)
    def _():
        attn_ref[:BLOCK] = early_ref[...]
        attn_ref[BLOCK:] = late_ref[...]

    place_weights(place_ref, weights, rows_ref)
    out_ref[...] = dot_nn(attn_ref[...], rows_ref[...].reshape(WIDTH, out_ref.shape[1])).astype(jnp.bfloat16)


def project(place, early, late, *weights):
    tile = 512
    piece = pl.BlockSpec((4, HEAD_DIM, tile), lambda i, *_: (0, 0, i))
    return pl.pallas_call(
        project_kernel,
        grid_spec=pltpu.PrefetchScalarGridSpec(
            num_scalar_prefetch=1,
            grid=(WIDTH // tile,),
            in_specs=[fixed((BLOCK, WIDTH)), fixed((BLOCK, WIDTH))] + [piece] * 4,
            out_specs=pl.BlockSpec((TOK, tile), lambda i, *_: (0, i)),
            scratch_shapes=[pltpu.VMEM((4, 2, 2, HEAD_DIM, tile), jnp.bfloat16), pltpu.VMEM((TOK, WIDTH), jnp.bfloat16)],
        ),
        out_shape=jax.ShapeDtypeStruct((TOK, WIDTH), jnp.bfloat16),
        compiler_params=params(),
        cost_estimate=cost(8e9),
        name="project",
    )(place, early, late, *weights)


def sum_pieces_kernel(pieces_ref, out_ref):
    total = pieces_ref[0].astype(jnp.float32)
    for i in range(1, pieces_ref.shape[0]):
        total += pieces_ref[i].astype(jnp.float32)
    total = total.astype(jnp.bfloat16)
    for i in range(out_ref.shape[0]):
        out_ref[i] = total


def sum_pieces(pieces, copies, tile):
    count, rows, width = pieces.shape
    return pl.pallas_call(
        sum_pieces_kernel,
        grid=(rows // tile,),
        in_specs=[pl.BlockSpec((count, tile, width), lambda i: (0, i, 0))],
        out_specs=pl.BlockSpec((copies, tile, width), lambda i: (0, i, 0)),
        out_shape=jax.ShapeDtypeStruct((copies, rows, width), jnp.bfloat16),
        compiler_params=params(),
        cost_estimate=cost(2e9),
        name="sum_pieces",
    )(pieces)


def swapped(array):
    return lax.ppermute(array, "core", [(0, 1), (1, 0)])


def passed_along(array, by):
    devices = 16
    pairs = [(i, i + by) for i in range(devices) if 0 <= i + by < devices]
    return lax.ppermute(array, GROUP_AXES, pairs)


def across_z(array):
    return lax.ppermute(array, ("zh", "zl"), [(z, 3 - z) for z in range(4)])


def tied(array, *others):
    return lax.optimization_barrier((array, *others))[0]


def on_device(query_rows, key_rows, value_rows, pyramid_start, scale_end, out_weight, cotangent):
    core = lax.axis_index("core").astype(jnp.int32)
    group_index = lax.axis_index(GROUP_AXES).astype(jnp.int32)
    core_arg = core.reshape(1)
    place = jnp.stack([core, lax.axis_index("zh").astype(jnp.int32)])
    start = (pyramid_start - group_index * TOK).reshape(1, TOK)
    end = (scale_end - group_index * TOK).reshape(1, TOK)

    half = lax.dynamic_slice_in_dim(out_weight, core * HEAD_DIM, HEAD_DIM, 0)
    near_halves = jnp.broadcast_to(half, (4, HEAD_DIM, WIDTH))
    near = lax.all_to_all(near_halves, "y", 0, 0, tiled=True)
    far_half = across_z(half)
    after_rows = jnp.concatenate([key_rows[:AFTER], value_rows[:AFTER]], axis=1)
    after_rows = tied(after_rows, near_halves)
    after = passed_along(after_rows, -1)
    before_rows = jnp.concatenate([key_rows[TOK - BEFORE:], value_rows[TOK - BEFORE:]], axis=1)
    before = passed_along(tied(before_rows, after_rows, after), 1)
    cot_peer = swapped(tied(cotangent, after_rows))
    far_halves = jnp.broadcast_to(far_half, (4, HEAD_DIM, WIDTH))

    late, late_theirs, late_lse = forward(
        True, core_arg, start, end, tied(query_rows, far_halves), key_rows, value_rows, after)
    far = lax.all_to_all(tied(far_halves, near, late), "y", 0, 0, tiled=True)
    peer_late = swapped(late_theirs)
    early, early_theirs, early_lse = forward(
        False, core_arg, start, end, tied(query_rows, peer_late), key_rows, value_rows, before)
    peer_early = swapped(early_theirs)
    near_other = swapped(tied(near, late))
    sums = weight_sums(core_arg, early, late, peer_early, peer_late, cotangent, tied(cot_peer, near_other))
    far = tied(far, sums)
    pieces = lax.all_to_all(tied(sums.reshape(4, 2 * HEAD_DIM, WIDTH), far), "y", 0, 0, tiled=True)
    far_other = swapped(far)
    weights = (near, far, near_other, far_other)
    grad_attn = grad_attention(place, tied(cotangent, far), *weights)
    shared = (start, end, early_lse, late_lse, query_rows, grad_attn, key_rows, value_rows, before, after)
    dq, dk, dv, to_previous, to_next = backward(0, *shared)
    from_next = [passed_along(to_previous, -1)]
    from_prev = [passed_along(to_next, 1)]
    dq, dk, dv, to_previous, to_next = backward(1, *shared, dq, dk, dv)
    from_next.append(passed_along(to_previous, -1))
    from_prev.append(passed_along(to_next, 1))

    partial = tied(sum_pieces(tied(pieces, dk), 1, 128), from_prev[0], from_next[0]).reshape(16, 16, WIDTH)
    shares = lax.all_to_all(partial, ("zh", "x", "zl"), 0, 0, tiled=True)
    layer_out = project(place, tied(early, partial, from_next[1]), late, *weights)
    summed = sum_pieces(tied(shares, layer_out), 8, 16)
    rows_mine = lax.all_to_all(summed, ("x", "zl"), 0, 0, tiled=True).reshape(HEAD_DIM, WIDTH)
    key_grad, value_grad = finish(tied(dk, summed), dv, from_prev, from_next)
    rows_mine = tied(rows_mine, key_grad)
    rows_other = swapped(rows_mine)
    first = jnp.where(core == 0, rows_mine, rows_other)
    second = jnp.where(core == 0, rows_other, rows_mine)
    weight_grad = jnp.concatenate([first, second], axis=0).astype(jnp.float32) * (float(TOKENS) ** -0.5)
    return (layer_out, dq, key_grad, value_grad, weight_grad)


def solution(mesh):
    inner = Mesh(mesh.devices.reshape(SIZES), AXES)
    rows = P(AXES, None)
    shard = P(("y", "zh"), None)
    return jax.shard_map(
        on_device,
        mesh=inner,
        in_specs=(rows, rows, rows, P(AXES), P(AXES), shard, rows),
        out_specs=(rows, rows, rows, rows, shard),
        check_vma=False,
    )
```
